512 devices in a mesh: wide: 128 (over y, x, z_lo), narrow: 4 (over z_hi, core).
Axes of the slice: x: 4, y: 8, z: 8 (z_hi: 2, z_lo: 4; z = z_hi * 4 + z_lo), core: 2. Of those that a mesh axis runs over, the one named last changes fastest.
Arguments:
- state_rhs: float32 [3, 1024, 128, 256], P(None, 'wide', 'narrow'), may hold values from -8 to 8
- adjoint_rhs: float32 [3, 1024, 128, 256], P(None, 'wide', 'narrow'), may hold values from -8 to 8
- penalty: float32 [1024, 128, 256], P('wide', 'narrow'), may hold values from 0.05 to 20
- margin_width: int32 [128, 4], P('wide', 'narrow'), may hold values from 1 to 3
- owner_map: int32 [128, 4], replicated, may hold values from 0 to 63
- coarse_inv: float32 [64, 64], replicated, may hold values from -1 to 1
Outputs:
- state_update: float32 [3, 1024, 128, 256], P(None, 'wide', 'narrow')
- adjoint_update: float32 [3, 1024, 128, 256], P(None, 'wide', 'narrow')
- sensitivity: float32 [1024, 128, 256], P('wide', 'narrow')
The draws below stay inside these ranges and needn't reach their ends.
All inputs are finite; a program needn't handle non-finite values. Where the reference program divides by a largest or mean magnitude, that divisor is 1e-20 or more.
Results may differ from the reference program's by a relative error of at most 0.00018.
Values sent between devices are 32-bit elements; how exact they have to be, the bound alone decides.
A program may use at most 64 MiB of HBM per device.

```python
import math
import jax
import jax.numpy as jnp
from jax import lax

CX = 8
CY = 32
OV = 3
SWEEPS = 4
NX = 1024
NY = 128
NZ = 256
GROUPS = 64
N_WIDE = 128
N_NARROW = 4


def rough_field(key, spread):
    noise_key, offset_key = jax.random.split(key, 2)
    offsets = jax.random.uniform(offset_key, (3, NX // CX, 1, NY // CY, 1, 1), jnp.float32, -spread, spread)
    offsets = jnp.broadcast_to(offsets, (3, NX // CX, CX, NY // CY, CY, NZ)).reshape(3, NX, NY, NZ)
    noise = jnp.clip(jax.random.normal(noise_key, (3, NX, NY, NZ), jnp.float32), -4.0, 4.0)
    return noise + offsets


def draw_state_rhs(key, part):
    key = jax.random.fold_in(key, 11)
    return rough_field(key, 1.5)


def draw_adjoint_rhs(key, part):
    key = jax.random.fold_in(key, 12)
    return rough_field(key, 1.5)


def draw_coarse_inv(key, part):
    key = jax.random.fold_in(key, 13)
    spread = 0.3
    entries = jax.random.uniform(key, (GROUPS, GROUPS), jnp.float32, -spread, spread) * GROUPS ** (-0.5)
    return entries + 0.6 * jnp.eye(GROUPS, dtype=jnp.float32)


def set_ends(values, own_key, least, high):
    shape = values.shape
    spot = [jax.random.randint(jax.random.fold_in(own_key, axis), (), 0, shape[axis]) for axis in range(len(shape))]
    values = values.at[tuple(spot)].set(least)
    longest = shape.index(max(shape))
    spot[longest] = (spot[longest] + 1) % shape[longest]
    return values.at[tuple(spot)].set(high)


def block_levels(rng, shape, cuts, least, top_value):
    loudness = 1.0
    for position, shards_of in cuts:
        steps = jax.random.uniform(jax.random.fold_in(jax.random.fold_in(rng, 6), position), (shards_of,), jnp.float32, least / len(cuts), top_value / len(cuts))
        loudness = loudness * jnp.repeat(jnp.exp(steps), shape[position] // shards_of).reshape((-1,) + (1,) * (len(shape) - 1 - position))
    return loudness


def setup_inputs(seed: int = 0) -> dict:
    streams_of = jax.random.split(jax.random.key(seed), 7)
    state_rhs = draw_state_rhs(jax.random.fold_in(streams_of[6], 71), 0)
    adjoint_rhs = draw_adjoint_rhs(jax.random.fold_in(streams_of[6], 71), 0)
    penalty = jnp.clip(jnp.exp(math.log(20.0) - 5.9914645 * jax.random.uniform(streams_of[2], (NX, NY, NZ), jnp.float32) ** block_levels(streams_of[2], (NX, NY, NZ), ((0, 128), (1, 4)), -0.2, 0.2)), 0.05, 20.0)
    margin_width = set_ends(jax.random.randint(streams_of[3], (N_WIDE, N_NARROW), 1, OV + 1), jax.random.fold_in(streams_of[3], 1), 1, OV).astype(jnp.int32)
    owner_map = set_ends(jax.random.randint(streams_of[4], (N_WIDE, N_NARROW), 0, GROUPS), jax.random.fold_in(streams_of[4], 1), 0, GROUPS - 1).astype(jnp.int32)
    coarse_inv = draw_coarse_inv(jax.random.fold_in(streams_of[6], 71), 0)
    return dict(state_rhs=state_rhs, adjoint_rhs=adjoint_rhs, penalty=penalty, margin_width=margin_width, owner_map=owner_map, coarse_inv=coarse_inv)


GRAD_DIV_WEIGHT = 1.0
DAMPING = 0.7
PEAK_EPS = 1e-6


def apply_operator(iterate, penalty_box):
    padded = jnp.pad(iterate, ((0, 0), (1, 1), (1, 1), (1, 1)))
    ext_a, ext_b, ext_c = iterate.shape[1], iterate.shape[2], iterate.shape[3]

    def shifted(c, step):
        return padded[c, 1 + step[0]:1 + step[0] + ext_a, 1 + step[1]:1 + step[1] + ext_b, 1 + step[2]:1 + step[2] + ext_c]

    unit_steps = ((1, 0, 0), (0, 1, 0), (0, 0, 1))
    result_rows = []
    for c in range(3):
        centre = iterate[c]
        beside = jnp.zeros_like(centre)
        for unit in unit_steps:
            beside = beside + shifted(c, unit) + shifted(c, tuple(-v for v in unit))
        own_unit = unit_steps[c]
        grad_div = shifted(c, own_unit) + shifted(c, tuple(-v for v in own_unit)) - 2.0 * centre
        for d in range(3):
            if d != c:
                other = unit_steps[d]
                plus_plus = tuple(own_unit[t] + other[t] for t in range(3))
                plus_minus = tuple(own_unit[t] - other[t] for t in range(3))
                grad_div = grad_div + 0.25 * (shifted(d, plus_plus) - shifted(d, plus_minus)
                                              - shifted(d, tuple(-v for v in plus_minus))
                                              + shifted(d, tuple(-v for v in plus_plus)))
        result_rows.append(6.0 * centre - beside + penalty_box * centre - GRAD_DIV_WEIGHT * grad_div)
    return jnp.stack(result_rows, 0)


def local_solve(source, penalty_box, inside):
    diagonal = 6.0 + penalty_box + 2.0 * GRAD_DIV_WEIGHT
    iterate = jnp.zeros_like(source)
    for iteration in range(SWEEPS):
        iterate = inside * (iterate + DAMPING * (source - apply_operator(iterate, penalty_box)) / diagonal)
    return iterate


def reference(state_rhs, adjoint_rhs, penalty, margin_width, owner_map, coarse_inv):
    n_sub = N_WIDE * N_NARROW
    wrapped = jnp.concatenate([state_rhs[:, NX - OV:], state_rhs, state_rhs[:, :OV]], 1)
    wrapped = jnp.pad(wrapped, ((0, 0), (0, 0), (OV, OV), (0, 0)))
    pen_wrap = jnp.concatenate([penalty[NX - OV:], penalty, penalty[:OV]], 0)
    pen_wrap = jnp.pad(pen_wrap, ((0, 0), (OV, OV), (0, 0)))
    box_x = CX + 2 * OV
    box_y = CY + 2 * OV
    row_x = jnp.arange(box_x, dtype=jnp.int32) - OV
    row_y = jnp.arange(box_y, dtype=jnp.int32) - OV
    zero_int = jnp.int32(0)

    def one_block(index, carry):
        state_out, gathered = carry
        block_i = (index // N_NARROW).astype(jnp.int32)
        block_j = (index % N_NARROW).astype(jnp.int32)
        start_x = block_i * CX
        start_y = block_j * CY
        reach_cells = margin_width[block_i, block_j]
        global_y = start_y + row_y
        in_x = (row_x >= -reach_cells) & (row_x < CX + reach_cells)
        in_y = (row_y >= -reach_cells) & (row_y < CY + reach_cells) & (global_y >= 0) & (global_y < NY)
        inside = (in_x[:, None] & in_y[None, :]).astype(jnp.float32)[:, :, None]
        source = lax.dynamic_slice(wrapped, (zero_int, start_x, start_y, zero_int), (3, box_x, box_y, NZ))
        penalty_box = lax.dynamic_slice(pen_wrap, (start_x, start_y, zero_int), (box_x, box_y, NZ))
        solved = local_solve(inside * source, penalty_box, inside)
        state_out = lax.dynamic_update_slice(state_out, solved[:, OV:OV + CX, OV:OV + CY], (zero_int, start_x, start_y, zero_int))
        own_adj = lax.dynamic_slice(adjoint_rhs, (zero_int, start_x, start_y, zero_int), (3, CX, CY, NZ))
        adj_source = jnp.pad(own_adj, ((0, 0), (OV, OV), (OV, OV), (0, 0)))
        adj_solved = local_solve(inside * adj_source, penalty_box, inside)
        current = lax.dynamic_slice(gathered, (zero_int, start_x, start_y, zero_int), (3, box_x, box_y, NZ))
        gathered = lax.dynamic_update_slice(gathered, current + adj_solved, (zero_int, start_x, start_y, zero_int))
        return state_out, gathered

    state_local = jnp.zeros((3, NX, NY, NZ), jnp.float32)
    gathered = jnp.zeros((3, NX + 2 * OV, NY + 2 * OV, NZ), jnp.float32)
    state_local, gathered = lax.fori_loop(0, n_sub, one_block, (state_local, gathered))
    gathered = gathered.at[:, NX:NX + OV].add(gathered[:, :OV])
    gathered = gathered.at[:, OV:2 * OV].add(gathered[:, NX + OV:])
    adjoint_local = gathered[:, OV:OV + NX, OV:OV + NY]

    state_means = state_rhs.reshape(3, N_WIDE, CX, N_NARROW, CY, NZ).mean(axis=(2, 4, 5)).reshape(3, n_sub)
    adj_means = adjoint_rhs.reshape(3, N_WIDE, CX, N_NARROW, CY, NZ).mean(axis=(2, 4, 5)).reshape(3, n_sub)
    block_means = jnp.concatenate([state_means, adj_means], 0)
    owner_flat = owner_map.reshape(-1)
    owner_table = (owner_flat[:, None] == jnp.arange(GROUPS, dtype=jnp.int32)[None, :]).astype(jnp.float32)
    highest = lax.Precision.HIGHEST
    coarse_rhs = jnp.dot(block_means, owner_table, precision=highest)
    state_coarse = jnp.dot(coarse_rhs[:3], coarse_inv.T, precision=highest)
    state_corr = jnp.dot(state_coarse, owner_table.T, precision=highest) - jnp.mean(state_coarse, axis=1, keepdims=True)
    centred = coarse_rhs[3:] - jnp.mean(coarse_rhs[3:], axis=1, keepdims=True)
    adjoint_coarse = jnp.dot(centred, coarse_inv, precision=highest)
    adj_corr = jnp.dot(adjoint_coarse, owner_table.T, precision=highest)

    state_update = (state_local.reshape(3, N_WIDE, CX, N_NARROW, CY, NZ)
                    + state_corr.reshape(3, N_WIDE, 1, N_NARROW, 1, 1)).reshape(3, NX, NY, NZ)
    adjoint_update = (adjoint_local.reshape(3, N_WIDE, CX, N_NARROW, CY, NZ)
                      + adj_corr.reshape(3, N_WIDE, 1, N_NARROW, 1, 1)).reshape(3, NX, NY, NZ)
    sens_raw = -jnp.sum(state_update * adjoint_update, axis=0)
    sensitivity = sens_raw / (jnp.max(jnp.abs(sens_raw)) + PEAK_EPS)
    return state_update, adjoint_update, sensitivity
```

```python
import functools

import jax
import jax.numpy as jnp
from jax import lax
from jax.experimental import pallas as pl
from jax.experimental.pallas import tpu as pltpu
from jax.sharding import PartitionSpec as P

MESH = pl.DeviceIdType.MESH
F32 = jnp.float32

OV = 3
CX = 8
CY = 32
LANES = 128
GROUPS = 64
W = 128
N = 4
DAMPING = 0.7
PEAK_EPS = 1e-06

XR = 16
YR = 48
X0 = 4
Y0 = 8
BOX_Y = 5
BOX_NY = 40
PEN, STATE = 0, 1


def zshift(v0, v1, lane):
    a0, a1 = pltpu.roll(v0, LANES - 1, 1), pltpu.roll(v1, LANES - 1, 1)
    b0, b1 = pltpu.roll(v0, 1, 1), pltpu.roll(v1, 1, 1)
    last, first = lane == LANES - 1, lane == 0
    return (
        (jnp.where(last, a1, a0), jnp.where(first, 0.0, b0)),
        (jnp.where(last, 0.0, a1), jnp.where(first, b0, b1)),
    )


def sweep(src, dst, source, gain, tx, ty, lo, hi):
    y0, ny = BOX_Y, BOX_NY
    lane = lax.broadcasted_iota(jnp.int32, (ny, LANES), 1)

    def at(ref, h, c, i, d=0):
        return ref[h, c, i, pl.ds(y0 + d, ny), :]

    def flat(ref, h, i, d=0):
        return ref[h, i, pl.ds(y0 + d, ny), :]

    def edge(i):
        for h, (plus, minus) in enumerate(zshift(at(src, 0, 2, i), at(src, 1, 2, i), lane)):
            q = at(src, h, 1, i, 1) - at(src, h, 1, i, -1)
            tx[h, i, pl.ds(y0, ny), :] = 0.25 * (q + (plus - minus))

    def first(i, carry):
        vz = [at(src, h, 2, i) for h in (0, 1)]
        mixed, sums = [], []
        for h, (plus, minus) in enumerate(zshift(vz[0], vz[1], lane)):
            p = at(src, h, 0, i + 1) - at(src, h, 0, i - 1)
            q = at(src, h, 1, i, 1) - at(src, h, 1, i, -1)
            r = plus - minus
            tx[h, i, pl.ds(y0, ny), :] = 0.25 * (q + r)
            ty[h, i, pl.ds(y0, ny), :] = 0.25 * (p + r)
            mixed.append(0.25 * (p + q))
            own = plus + minus
            sums.append(
                (own + own)
                + (at(src, h, 2, i + 1) + at(src, h, 2, i - 1))
                + (at(src, h, 2, i, 1) + at(src, h, 2, i, -1))
            )
        for h, (plus, minus) in enumerate(zshift(mixed[0], mixed[1], lane)):
            total = at(source, h, 2, i) + (sums[h] + (plus - minus))
            dst[h, 2, i, pl.ds(y0, ny), :] = 0.3 * vz[h] + flat(gain, h, i) * total
        return carry

    def second(i, carry):
        vx = [at(src, h, 0, i) for h in (0, 1)]
        vy = [at(src, h, 1, i) for h in (0, 1)]
        zx = zshift(vx[0], vx[1], lane)
        zy = zshift(vy[0], vy[1], lane)
        for h in (0, 1):
            g = flat(gain, h, i)
            own = at(src, h, 0, i + 1) + at(src, h, 0, i - 1)
            total = (
                (own + own)
                + (at(src, h, 0, i, 1) + at(src, h, 0, i, -1))
                + (zx[h][0] + zx[h][1])
                + (flat(tx, h, i + 1) - flat(tx, h, i - 1))
            )
            dst[h, 0, i, pl.ds(y0, ny), :] = 0.3 * vx[h] + g * (at(source, h, 0, i) + total)
            own = at(src, h, 1, i, 1) + at(src, h, 1, i, -1)
            total = (
                (own + own)
                + (at(src, h, 1, i + 1) + at(src, h, 1, i - 1))
                + (zy[h][0] + zy[h][1])
                + (flat(ty, h, i, 1) - flat(ty, h, i, -1))
            )
            dst[h, 1, i, pl.ds(y0, ny), :] = 0.3 * vy[h] + g * (at(source, h, 1, i) + total)
        return carry

    edge(lo - 1)
    edge(hi + 1)
    lax.fori_loop(lo, hi + 1, first, 0)
    lax.fori_loop(lo, hi + 1, second, 0)


def zero(ref):
    lead = ref.shape[:-3]
    rows = ref.shape[-2:]

    def one(i, carry):
        for h in range(lead[0]):
            if len(lead) == 1:
                ref[h, i] = jnp.zeros(rows, F32)
            else:
                for c in range(lead[1]):
                    ref[h, c, i] = jnp.zeros(rows, F32)
        return carry

    lax.fori_loop(0, ref.shape[-3], one, 0)


def zero_margins(ref):
    def one(i, carry):
        for h in (0, 1):
            for y in (0, Y0 + CY):
                if len(ref.shape) == 4:
                    ref[h, i, pl.ds(y, 8), :] = jnp.zeros((8, LANES), F32)
                else:
                    for c in range(3):
                        ref[h, c, i, pl.ds(y, 8), :] = jnp.zeros((8, LANES), F32)
        return carry

    lax.fori_loop(0, XR, one, 0)


def kernel(
    state,
    adjoint,
    penalty,
    margin,
    owner,
    inverse,
    state_out,
    adjoint_out,
    sens_out,
    s_src,
    a_src,
    s_a,
    s_b,
    a_a,
    a_b,
    pen,
    gain,
    tx,
    ty,
    py_out,
    py_in,
    pc_out,
    pc_in,
    sy_out,
    sy_in,
    sc_out,
    sc_in,
    ay_out,
    ay_in,
    ax_in,
    red,
    corr,
    load_sem,
    x_send,
    x_recv,
    y_send,
    y_recv,
    r_send,
    r_recv,
):
    w, n = lax.axis_index("wide"), lax.axis_index("narrow")
    py, px, pz = w // 16, lax.rem(w // 4, 4), lax.rem(w, 4)
    ph, pc = n // 2, lax.rem(n, 2)
    left, right = lax.rem(w + W - 1, W), lax.rem(w + 1, W)
    down, up = lax.rem(n + N - 1, N), lax.rem(n + 1, N)
    stages = (
        [(lax.rem(py + k, 8) * 16 + px * 4 + pz, n) for k in range(1, 8)],
        [
            (py * 16 + lax.rem(px + k // 2, 4) * 4 + pz, ph * 2 + lax.rem(pc + k % 2, 2))
            for k in range(1, 8)
        ],
        [
            (py * 16 + px * 4 + lax.rem(pz + k // 2, 4), lax.rem(ph + k % 2, 2) * 2 + pc)
            for k in range(1, 8)
        ],
    )
    has_down, has_up = n > 0, n < N - 1

    barrier = pltpu.get_barrier_semaphore()
    for device in [(left, n), (right, n)] + stages[0] + stages[1] + stages[2]:
        pl.semaphore_signal(barrier, inc=1, device_id=device, device_id_type=MESH)

    @pl.when(has_down)
    def _():
        pl.semaphore_signal(barrier, inc=1, device_id=(w, down), device_id_type=MESH)

    @pl.when(has_up)
    def _():
        pl.semaphore_signal(barrier, inc=1, device_id=(w, up), device_id_type=MESH)

    loads = []
    for h in (0, 1):
        z = pl.ds(h * LANES, LANES)
        own_x, own_y = pl.ds(X0, CX), pl.ds(Y0, CY)
        for k, (ref, target) in enumerate(
            (
                (penalty.at[:, :, z], pen.at[h, own_x, own_y, :]),
                (adjoint.at[:, :, :, z], a_src.at[h, :, own_x, own_y, :]),
                (state.at[:, :, :, z], s_src.at[h, :, own_x, own_y, :]),
            )
        ):
            copy = pltpu.make_async_copy(ref, target, load_sem.at[2 * k + h])
            copy.start()
            loads.append(copy)

    zero_margins(pen)
    zero_margins(s_src)
    zero_margins(a_src)
    for ref in (s_a, s_b, a_a, a_b, tx, ty):
        zero(ref)
    for h in (0, 1):
        for c in range(3):
            for x in (0, 1, 2, 3, 12, 13, 14, 15):
                a_src[h, c, x, pl.ds(Y0, CY), :] = jnp.zeros((CY, LANES), F32)

    peers = 23 + has_down.astype(jnp.int32) + has_up.astype(jnp.int32)
    pl.semaphore_wait(barrier, peers)

    def x_copy(which, d, h):
        rows, target = (pl.ds(0, OV), pl.ds(12, OV)) if d == 0 else (pl.ds(CX - OV, OV), pl.ds(1, OV))
        z, own_y = pl.ds(h * LANES, LANES), pl.ds(Y0, CY)
        if which == PEN:
            ref, to = penalty.at[rows, :, z], pen.at[h, target, own_y, :]
        else:
            ref, to = state.at[:, rows, :, z], s_src.at[h, :, target, own_y, :]
        return pltpu.make_async_remote_copy(
            src_ref=ref,
            dst_ref=to,
            send_sem=x_send.at[4 * which + 2 * d + h],
            recv_sem=x_recv.at[4 * which + 2 * (1 - d) + h],
            device_id=(left if d == 0 else right, n),
            device_id_type=MESH,
        )

    def adjoint_copy(d, h):
        rows = pl.ds(1, OV) if d == 0 else pl.ds(12, OV)
        return pltpu.make_async_remote_copy(
            src_ref=a_b.at[h, :, rows, pl.ds(Y0, CY), :],
            dst_ref=ax_in.at[1 - d, h],
            send_sem=x_send.at[8 + 2 * d + h],
            recv_sem=x_recv.at[8 + 2 * (1 - d) + h],
            device_id=(left if d == 0 else right, n),
            device_id_type=MESH,
        )

    both = [(d, h) for d in (0, 1) for h in (0, 1)]
    for which in (PEN, STATE):
        for d, h in both:
            x_copy(which, d, h).start()

    def y_copy(message, d):
        out, land = ((py_out, py_in), (pc_out, pc_in), (sy_out, sy_in), (sc_out, sc_in), (ay_out, ay_in))[
            message
        ]
        return pltpu.make_async_remote_copy(
            src_ref=out.at[d],
            dst_ref=land.at[1 - d],
            send_sem=y_send.at[2 * message + d],
            recv_sem=y_recv.at[2 * message + 1 - d],
            device_id=(w, down if d == 0 else up),
            device_id_type=MESH,
        )

    def each_side(action):
        @pl.when(has_down)
        def _():
            action(0)

        @pl.when(has_up)
        def _():
            action(1)

    def y_send_now(message):
        each_side(lambda d: y_copy(message, d).start())

    inner = (Y0, Y0 + CY - OV)
    outer = (Y0 - OV, Y0 + CY)

    def rows_of(ref, h, c, i, y):
        return ref.at[h, i, pl.ds(y, OV), :] if c is None else ref.at[h, c, i, pl.ds(y, OV), :]

    def moves(blocks, comps, step):
        width = sum(count for _, count in blocks)
        base = 0
        for start, count in blocks:

            def one(k, carry, start=start, base=base):
                for h in (0, 1):
                    for j, c in enumerate(comps):
                        step(h, c, start + k, pl.ds((j * width + base + k) * OV, OV))
                return carry

            lax.fori_loop(0, count, one, 0)
            base += count

    def pack(ref, out, blocks, comps, d, ys):
        def step(h, c, i, slot):
            out[d, h, slot, :] = rows_of(ref, h, c, i, ys[d])[...]

        moves(blocks, comps, step)

    def unpack(ref, land, blocks, comps, d, ys, add=False):
        def step(h, c, i, slot):
            cell = rows_of(ref, h, c, i, ys[d])
            cell[...] = cell[...] + land[d, h, slot, :] if add else land[d, h, slot, :]

        moves(blocks, comps, step)

    own_rows = ((X0, CX),)
    rim_rows = ((1, OV), (12, OV))
    box_rows = ((1, CX + 2 * OV),)
    pen_comps, all_comps = (None,), (0, 1, 2)

    def reduce_copy(use, s, k):
        slot = (use * 3 + s) * 8
        return pltpu.make_async_remote_copy(
            src_ref=red.at[slot],
            dst_ref=red.at[slot + k],
            send_sem=r_send.at[slot + k],
            recv_sem=r_recv.at[slot + k],
            device_id=stages[s][k - 1],
            device_id_type=MESH,
        )

    def reduce_start(use, s, value):
        red[(use * 3 + s) * 8] = value
        for k in range(1, 8):
            reduce_copy(use, s, k).start()

    def reduce_finish(use, s, combine):
        for k in range(1, 8):
            reduce_copy(use, s, k).wait_recv()
        slot = (use * 3 + s) * 8
        value = [red[slot + k] for k in range(8)]
        while len(value) > 1:
            value = [combine(value[2 * k], value[2 * k + 1]) for k in range(len(value) // 2)]
        return value[0]

    for copy in loads:
        copy.wait()

    each_side(lambda d: pack(pen, py_out, own_rows, pen_comps, d, inner))
    y_send_now(0)
    each_side(lambda d: pack(s_src, sy_out, own_rows, all_comps, d, inner))
    y_send_now(2)

    spot = (lax.broadcasted_iota(jnp.int32, (N, W), 0) == n) & (
        lax.broadcasted_iota(jnp.int32, (N, W), 1) == w
    )
    own_group = jnp.sum(jnp.where(spot, owner[...].astype(F32), 0.0), axis=(0, 1), keepdims=True)
    pick = (lax.broadcasted_iota(jnp.int32, (1, LANES), 1).astype(F32) == own_group).astype(F32)
    row = lax.broadcasted_iota(jnp.int32, (8, LANES), 0)
    sums = jnp.zeros((8, LANES), F32)
    for k, ref in enumerate((s_src, a_src)):
        for c in range(3):

            def add(i, total, ref=ref, c=c):
                cells = ref[0, c, i, pl.ds(Y0, CY), :] + ref[1, c, i, pl.ds(Y0, CY), :]
                return total + ((cells[0:8] + cells[8:16]) + (cells[16:24] + cells[24:32]))

            total = lax.fori_loop(X0, X0 + CX, add, jnp.zeros((8, LANES), F32))
            mean = jnp.sum(total, axis=(0, 1), keepdims=True) * (1.0 / (CX * CY * 2 * LANES))
            sums = sums + jnp.where(row == 3 * k + c, mean * pick, 0.0)
    reduce_start(0, 0, sums)

    for d, h in both:
        x_copy(PEN, d, h).wait_recv()
    each_side(lambda d: pack(pen, pc_out, rim_rows, pen_comps, d, inner))
    y_send_now(1)

    width = margin[0, 0]
    column = lax.broadcasted_iota(jnp.int32, (BOX_NY, LANES), 0) + (BOX_Y - Y0)
    place = column + n * CY
    in_y = (column >= -width) & (column < CY + width) & (place >= 0) & (place < N * CY)

    def y_arrived(message, d):
        y_copy(message, 1 - d).wait_recv()

    each_side(lambda d: y_arrived(0, d))
    each_side(lambda d: unpack(pen, py_in, own_rows, pen_comps, d, outer))
    each_side(lambda d: y_arrived(1, d))
    each_side(lambda d: unpack(pen, pc_in, rim_rows, pen_comps, d, outer))

    def set_gain(i, carry):
        line = jnp.zeros((BOX_NY, LANES), jnp.int32) + (i - X0)
        inside = in_y & (line >= -width) & (line < CX + width)
        for h in (0, 1):
            value = DAMPING / (8.0 + pen[h, i, pl.ds(BOX_Y, BOX_NY), :])
            gain[h, i, pl.ds(BOX_Y, BOX_NY), :] = jnp.where(inside, value, 0.0)
        return carry

    lax.fori_loop(1, XR - 1, set_gain, 0)

    def adjoint_first(i, carry):
        for h in (0, 1):
            g = gain[h, i, pl.ds(Y0, CY), :]
            for c in range(3):
                a_a[h, c, i, pl.ds(Y0, CY), :] = g * a_src[h, c, i, pl.ds(Y0, CY), :]
        return carry

    lax.fori_loop(X0, X0 + CX, adjoint_first, 0)
    sweep(a_a, a_b, a_src, gain, tx, ty, 3, 12)
    total = reduce_finish(0, 0, jnp.add)
    reduce_start(0, 1, total)
    sweep(a_b, a_a, a_src, gain, tx, ty, 2, 13)
    total = reduce_finish(0, 1, jnp.add)
    reduce_start(0, 2, total)
    sweep(a_a, a_b, a_src, gain, tx, ty, 1, 14)

    each_side(lambda d: pack(a_b, ay_out, box_rows, all_comps, d, outer))
    y_send_now(4)

    for d, h in both:
        x_copy(STATE, d, h).wait_recv()
    each_side(lambda d: pack(s_src, sc_out, rim_rows, all_comps, d, inner))
    y_send_now(3)

    each_side(lambda d: y_arrived(4, d))
    each_side(lambda d: unpack(a_b, ay_in, box_rows, all_comps, d, inner, add=True))
    for d, h in both:
        adjoint_copy(d, h).start()

    coarse = reduce_finish(0, 2, jnp.add)
    inv = inverse[...]
    across = lax.broadcasted_iota(jnp.int32, (GROUPS, GROUPS), 1)
    along = lax.broadcasted_iota(jnp.int32, (GROUPS, GROUPS), 0)
    rhs = coarse[:, :GROUPS]
    state_row = jnp.sum(
        ((along.astype(F32) == own_group).astype(F32) - 1.0 / GROUPS) * inv, axis=0, keepdims=True
    )
    adjoint_column = jnp.sum(
        (across.astype(F32) == own_group).astype(F32) * inv, axis=1, keepdims=True
    )
    adjoint_row = jnp.sum(jnp.where(along == across, adjoint_column, 0.0), axis=0, keepdims=True)
    centred = rhs - jnp.sum(rhs, axis=1, keepdims=True) * (1.0 / GROUPS)
    by_state = jnp.sum(rhs * state_row, axis=1, keepdims=True)
    by_adjoint = jnp.sum(centred * adjoint_row, axis=1, keepdims=True)
    corr[...] = jnp.where(row < 3, by_state, by_adjoint)

    for message in (2, 3):
        blocks = own_rows if message == 2 else rim_rows
        land = sy_in if message == 2 else sc_in
        each_side(lambda d, message=message: y_arrived(message, d))
        each_side(lambda d, blocks=blocks, land=land: unpack(s_src, land, blocks, all_comps, d, outer))

    def state_first(i, carry):
        for h in (0, 1):
            g = gain[h, i, pl.ds(BOX_Y, BOX_NY), :]
            for c in range(3):
                s_a[h, c, i, pl.ds(BOX_Y, BOX_NY), :] = g * s_src[h, c, i, pl.ds(BOX_Y, BOX_NY), :]
        return carry

    lax.fori_loop(1, XR - 1, state_first, 0)
    sweep(s_a, s_b, s_src, gain, tx, ty, 2, 13)
    sweep(s_b, s_a, s_src, gain, tx, ty, 3, 12)
    sweep(s_a, s_b, s_src, gain, tx, ty, 4, 11)

    for d, h in both:
        adjoint_copy(d, h).wait_recv()

    def add_shares(k, carry):
        for h in (0, 1):
            for c in range(3):
                for d, x in ((0, X0), (1, X0 + CX - OV)):
                    a_b[h, c, x + k, pl.ds(Y0, CY), :] = (
                        a_b[h, c, x + k, pl.ds(Y0, CY), :] + ax_in[d, h, c, k]
                    )
        return carry

    for d, h in both:
        adjoint_copy(d, h).wait_send()
    lax.fori_loop(0, OV, add_shares, 0)

    def finish(i, peak):
        for h in (0, 1):
            z = slice(h * LANES, (h + 1) * LANES)
            raw = None
            for c in range(3):
                s = s_b[h, c, X0 + i, pl.ds(Y0, CY), :] + corr[pl.ds(c, 1), :]
                a = a_b[h, c, X0 + i, pl.ds(Y0, CY), :] + corr[pl.ds(c + 3, 1), :]
                state_out[c, i, :, z] = s
                adjoint_out[c, i, :, z] = a
                raw = s * a if raw is None else raw + s * a
            sens_out[i, :, z] = -raw
            size = jnp.abs(raw)
            peak = jnp.maximum(
                peak,
                jnp.maximum(jnp.maximum(size[0:8], size[8:16]), jnp.maximum(size[16:24], size[24:32])),
            )
        return peak

    peak = lax.fori_loop(0, CX, finish, jnp.zeros((8, LANES), F32))
    for s in range(3):
        reduce_start(1, s, peak)
        peak = reduce_finish(1, s, jnp.maximum)
    scale = 1.0 / (jnp.max(peak, axis=(0, 1), keepdims=True) + PEAK_EPS)

    def normalise(i, carry):
        sens_out[i] = sens_out[i] * scale
        return carry

    lax.fori_loop(0, CX, normalise, 0)

    for which in (PEN, STATE):
        for d, h in both:
            x_copy(which, d, h).wait_send()
    for message in range(5):
        each_side(lambda d, message=message: y_copy(message, d).wait_send())
    for use in (0, 1):
        for s in range(3):
            for k in range(1, 8):
                reduce_copy(use, s, k).wait_send()


def body(state_rhs, adjoint_rhs, penalty, margin_width, owner_map, coarse_inv):
    vmem = pltpu.VMEM
    field = vmem((2, 3, XR, YR, LANES), F32)
    flat = vmem((2, XR, YR, LANES), F32)

    def message(rows):
        return [vmem((2, 2, rows, LANES), F32)] * 2

    dma = pltpu.SemaphoreType.DMA
    return pl.pallas_call(
        kernel,
        out_shape=(
            jax.ShapeDtypeStruct(state_rhs.shape, F32),
            jax.ShapeDtypeStruct(adjoint_rhs.shape, F32),
            jax.ShapeDtypeStruct(penalty.shape, F32),
        ),
        in_specs=[pl.BlockSpec(memory_space=pl.ANY)] * 3
        + [pl.BlockSpec(memory_space=pltpu.SMEM)]
        + [pl.BlockSpec(memory_space=vmem)] * 2,
        out_specs=(pl.BlockSpec(memory_space=vmem),) * 3,
        scratch_shapes=[field] * 6
        + [flat] * 4
        + message(24)
        + message(24)
        + message(72)
        + message(56)
        + message(128)
        + [
            vmem((2, 2, 3, OV, CY, LANES), F32),
            vmem((48, 8, LANES), F32),
            vmem((8, LANES), F32),
            dma((6,)),
            dma((12,)),
            dma((12,)),
            dma((10,)),
            dma((10,)),
            dma((48,)),
            dma((48,)),
        ],
        compiler_params=pltpu.CompilerParams(
            collective_id=0, has_side_effects=True, vmem_limit_bytes=60 * 1024 * 1024
        ),
        name="schwarz",
    )(state_rhs, adjoint_rhs, penalty, margin_width, owner_map.T, coarse_inv)


def solution(mesh):
    placed = (
        P(None, "wide", "narrow", None),
        P(None, "wide", "narrow", None),
        P("wide", "narrow", None),
        P("wide", "narrow"),
        P(),
        P(),
    )
    return jax.shard_map(
        body,
        mesh=mesh,
        in_specs=placed,
        out_specs=(
            P(None, "wide", "narrow", None),
            P(None, "wide", "narrow", None),
            P("wide", "narrow", None),
        ),
        check_vma=False,
    )
```

```python
import functools

import jax
import jax.numpy as jnp
from jax import lax
from jax.experimental import pallas as pl
from jax.experimental.pallas import tpu as pltpu
from jax.sharding import PartitionSpec as P

MESH = pl.DeviceIdType.MESH
F32 = jnp.float32

OV = 3
CX = 8
CY = 32
LANES = 128
GROUPS = 64
W = 128
N = 4
DAMPING = 0.7
PEAK_EPS = 1e-06

XR = 16
YR = 48
X0 = 4
Y0 = 8
BOX_Y = 5
BOX_NY = 40
PEN, STATE = 0, 1


def next_and_previous(plus, minus, lane):
    a0, a1 = pltpu.roll(plus[0], LANES - 1, 1), pltpu.roll(plus[1], LANES - 1, 1)
    b0, b1 = pltpu.roll(minus[0], 1, 1), pltpu.roll(minus[1], 1, 1)
    last, first = lane == LANES - 1, lane == 0
    return (
        jnp.where(last, a1, a0) + jnp.where(first, 0.0, b0),
        jnp.where(last, 0.0, a1) + jnp.where(first, b0, b1),
    )


def sweep(src, dst, source, gain, lo, hi, y0=BOX_Y, ny=BOX_NY):
    lane = lax.broadcasted_iota(jnp.int32, (ny, LANES), 1)

    def line(i, carry):
        centre, plus, minus, rest = [], [], [], []
        for h in (0, 1):

            def at(c, di=0, dy=0, h=h):
                return src[h, c, i + di, pl.ds(y0 + dy, ny), :]

            x0, x1, x2 = at(0), at(0, 1), at(0, -1)
            y_0, y1, y2 = at(1), at(1, 0, 1), at(1, 0, -1)
            z0 = at(2)
            xz = 0.25 * (at(2, 1) - at(2, -1))
            yz = 0.25 * (at(2, 0, 1) - at(2, 0, -1))
            zz = 0.25 * ((x1 - x2) + (y1 - y2))
            twice = z0 + z0
            centre.append((x0, y_0, z0))
            plus.append((x0 + xz, y_0 + yz, twice + zz))
            minus.append((x0 - xz, y_0 - yz, twice - zz))
            own_x, own_y = x1 + x2, y1 + y2
            rest.append(
                (
                    (own_x + own_x)
                    + (at(0, 0, 1) + at(0, 0, -1))
                    + 0.25 * ((at(1, 1, 1) - at(1, 1, -1)) - (at(1, -1, 1) - at(1, -1, -1))),
                    (own_y + own_y)
                    + (at(1, 1) + at(1, -1))
                    + 0.25 * ((at(0, 1, 1) - at(0, 1, -1)) - (at(0, -1, 1) - at(0, -1, -1))),
                    (at(2, 1) + at(2, -1)) + (at(2, 0, 1) + at(2, 0, -1)),
                )
            )
        for c in range(3):
            along = next_and_previous((plus[0][c], plus[1][c]), (minus[0][c], minus[1][c]), lane)
            for h in (0, 1):
                total = source[h, c, i, pl.ds(y0, ny), :] + (rest[h][c] + along[h])
                g = gain[h, i, pl.ds(y0, ny), :]
                dst[h, c, i, pl.ds(y0, ny), :] = 0.3 * centre[h][c] + g * total
        return carry

    lax.fori_loop(lo, hi + 1, line, 0)


def zero_rows(ref, rows):
    for i in rows:
        for h in (0, 1):
            for c in range(3):
                ref[h, c, i] = jnp.zeros((YR, LANES), F32)


def zero_margins(ref):
    def one(i, carry):
        for h in (0, 1):
            for y in (0, Y0 + CY):
                if len(ref.shape) == 4:
                    ref[h, i, pl.ds(y, 8), :] = jnp.zeros((8, LANES), F32)
                else:
                    for c in range(3):
                        ref[h, c, i, pl.ds(y, 8), :] = jnp.zeros((8, LANES), F32)
        return carry

    lax.fori_loop(0, XR, one, 0)


def kernel(
    state,
    adjoint,
    penalty,
    margin,
    owner,
    inverse,
    state_out,
    adjoint_out,
    sens_out,
    s_src,
    a_src,
    s_a,
    s_b,
    a_a,
    a_b,
    pen,
    gain,
    py_out,
    py_in,
    pc_in,
    sy_out,
    sy_in,
    sc_out,
    sc_in,
    ay_out,
    ay_in,
    ac_out,
    ac_in,
    ax_in,
    total_red,
    peak_red,
    corr,
    load_sem,
    x_send,
    x_recv,
    y_send,
    y_recv,
    r_send,
    r_recv,
):
    w, n = lax.axis_index("wide"), lax.axis_index("narrow")
    py, px, pz = w // 16, lax.rem(w // 4, 4), lax.rem(w, 4)
    ph, pc = n // 2, lax.rem(n, 2)
    left, right = lax.rem(w + W - 1, W), lax.rem(w + 1, W)
    down, up = lax.rem(n + N - 1, N), lax.rem(n + 1, N)
    stages = (
        [
            (py * 16 + px * 4 + lax.rem(pz + k // 4, 4), lax.rem(ph + k // 2 % 2, 2) * 2 + lax.rem(pc + k % 2, 2))
            for k in range(1, 16)
        ],
        [(lax.rem(py + k // 4, 8) * 16 + lax.rem(px + k % 4, 4) * 4 + pz, n) for k in range(1, 32)],
    )
    has_down, has_up = n > 0, n < N - 1

    barrier = pltpu.get_barrier_semaphore()
    for device in [(left, n), (right, n)] + stages[0] + stages[1]:
        pl.semaphore_signal(barrier, inc=1, device_id=device, device_id_type=MESH)

    @pl.when(has_down)
    def _():
        for at in (left, w, right):
            pl.semaphore_signal(barrier, inc=1, device_id=(at, down), device_id_type=MESH)

    @pl.when(has_up)
    def _():
        for at in (left, w, right):
            pl.semaphore_signal(barrier, inc=1, device_id=(at, up), device_id_type=MESH)

    loads = []
    own_x, own_y = pl.ds(X0, CX), pl.ds(Y0, CY)
    for k in range(3):
        for h in (0, 1):
            z = pl.ds(h * LANES, LANES)
            ref, target = (
                (penalty.at[:, :, z], pen.at[h, own_x, own_y, :]),
                (adjoint.at[:, :, :, z], a_src.at[h, :, own_x, own_y, :]),
                (state.at[:, :, :, z], s_src.at[h, :, own_x, own_y, :]),
            )[k]
            copy = pltpu.make_async_copy(ref, target, load_sem.at[2 * k + h])
            copy.start()
            loads.append(copy)

    zero_margins(s_src)
    peers = 48 + 3 * (has_down.astype(jnp.int32) + has_up.astype(jnp.int32))
    pl.semaphore_wait(barrier, peers)

    def x_copy(which, d, h):
        rows, target = (pl.ds(0, OV), pl.ds(12, OV)) if d == 0 else (pl.ds(CX - OV, OV), pl.ds(1, OV))
        z, own_y = pl.ds(h * LANES, LANES), pl.ds(Y0, CY)
        if which == PEN:
            ref, to = penalty.at[rows, :, z], pen.at[h, target, own_y, :]
        else:
            ref, to = state.at[:, rows, :, z], s_src.at[h, :, target, own_y, :]
        return pltpu.make_async_remote_copy(
            src_ref=ref,
            dst_ref=to,
            send_sem=x_send.at[4 * which + 2 * d + h],
            recv_sem=x_recv.at[4 * which + 2 * (1 - d) + h],
            device_id=(left if d == 0 else right, n),
            device_id_type=MESH,
        )

    def adjoint_copy(d, h):
        rows = pl.ds(1, OV) if d == 0 else pl.ds(12, OV)
        return pltpu.make_async_remote_copy(
            src_ref=a_b.at[h, :, rows, pl.ds(Y0, CY), :],
            dst_ref=ax_in.at[1 - d, h],
            send_sem=x_send.at[8 + 2 * d + h],
            recv_sem=x_recv.at[8 + 2 * (1 - d) + h],
            device_id=(left if d == 0 else right, n),
            device_id_type=MESH,
        )

    both = [(d, h) for d in (0, 1) for h in (0, 1)]
    for d, h in both:
        x_copy(PEN, d, h).start()

    def y_copy(message, d):
        out, land, rows, side = messages[message]
        return pltpu.make_async_remote_copy(
            src_ref=out.at[d, :, rows, :],
            dst_ref=land.at[1 - d, :, rows, :] if side == 0 else land.at[1 - d, 2 - side],
            send_sem=y_send.at[2 * message + d],
            recv_sem=y_recv.at[2 * message + 1 - d],
            device_id=((w, left, right)[side], down if d == 0 else up),
            device_id_type=MESH,
        )

    messages = (
        (py_out, py_in, pl.ds(0, 24), 0),
        (py_out, pc_in, pl.ds(0, 16), 1),
        (py_out, pc_in, pl.ds(8, 16), 2),
        (sy_out, sy_in, pl.ds(0, 72), 0),
        (sc_out, sc_in, pl.ds(0, 56), 0),
        (ay_out, ay_in, pl.ds(0, 72), 0),
        (ac_out, ac_in, pl.ds(0, 32), 1),
        (ac_out, ac_in, pl.ds(32, 32), 2),
    )

    def each_side(action):
        @pl.when(has_down)
        def _():
            action(0)

        @pl.when(has_up)
        def _():
            action(1)

    def y_send_now(message):
        each_side(lambda d: y_copy(message, d).start())

    inner = (Y0, Y0 + CY - OV)
    outer = (Y0 - OV, Y0 + CY)

    def rows_of(ref, h, c, i, y):
        return ref.at[h, i, pl.ds(y, OV), :] if c is None else ref.at[h, c, i, pl.ds(y, OV), :]

    def pack(ref, out, start, count, comps, d, ys, base=0):
        def step(k, carry):
            for h in (0, 1):
                for j, c in enumerate(comps):
                    slot = pl.ds(base + (k * len(comps) + j) * OV, OV)
                    out[d, h, slot, :] = rows_of(ref, h, c, start + k, ys[d])[...]
            return carry

        lax.fori_loop(0, count, step, 0)

    def unpack(ref, land, start, count, comps, y, base=0, add=False):
        def step(k, carry):
            for h in (0, 1):
                for j, c in enumerate(comps):
                    slot = pl.ds(base + (k * len(comps) + j) * OV, OV)
                    cell = rows_of(ref, h, c, start + k, y)
                    cell[...] = cell[...] + land[h, slot, :] if add else land[h, slot, :]
            return carry

        lax.fori_loop(0, count, step, 0)

    pen_comps, all_comps = (None,), (0, 1, 2)

    def reduce_copy(use, s, k):
        buffer, base = (total_red, peak_red)[use], 16 * s
        slot = 48 * use + base
        return pltpu.make_async_remote_copy(
            src_ref=buffer.at[base],
            dst_ref=buffer.at[base + k],
            send_sem=r_send.at[slot + k],
            recv_sem=r_recv.at[slot + k],
            device_id=stages[s][k - 1],
            device_id_type=MESH,
        )

    def reduce_start(use, s, value):
        (total_red, peak_red)[use][16 * s] = value
        for k in range(1, len(stages[s]) + 1):
            reduce_copy(use, s, k).start()

    def reduce_finish(use, s, combine):
        for k in range(1, len(stages[s]) + 1):
            reduce_copy(use, s, k).wait_recv()
        value = [(total_red, peak_red)[use][16 * s + k] for k in range(len(stages[s]) + 1)]
        while len(value) > 1:
            value = [combine(value[2 * k], value[2 * k + 1]) for k in range(len(value) // 2)]
        return value[0]

    for copy in loads[:2]:
        copy.wait()
    each_side(lambda d: pack(pen, py_out, X0, CX, pen_comps, d, inner))
    for message in (0, 1, 2):
        y_send_now(message)
    for copy in loads[2:]:
        copy.wait()

    spot = (lax.broadcasted_iota(jnp.int32, (N, W), 0) == n) & (
        lax.broadcasted_iota(jnp.int32, (N, W), 1) == w
    )
    own_group = jnp.sum(jnp.where(spot, owner[...].astype(F32), 0.0), axis=(0, 1), keepdims=True)
    pick = (lax.broadcasted_iota(jnp.int32, (1, LANES), 1).astype(F32) == own_group).astype(F32)
    row = lax.broadcasted_iota(jnp.int32, (8, LANES), 0)
    sums = jnp.zeros((8, LANES), F32)
    for k, ref in enumerate((s_src, a_src)):
        for c in range(3):

            def add(i, total, ref=ref, c=c):
                cells = ref[0, c, i, pl.ds(Y0, CY), :] + ref[1, c, i, pl.ds(Y0, CY), :]
                return total + ((cells[0:8] + cells[8:16]) + (cells[16:24] + cells[24:32]))

            total = lax.fori_loop(X0, X0 + CX, add, jnp.zeros((8, LANES), F32))
            mean = jnp.sum(total, axis=(0, 1), keepdims=True) * (1.0 / (CX * CY * 2 * LANES))
            sums = sums + jnp.where(row == 3 * k + c, mean * pick, 0.0)
    reduce_start(0, 0, sums)

    for d, h in both:
        x_copy(STATE, d, h).start()
    each_side(lambda d: pack(s_src, sy_out, X0, CX, all_comps, d, inner))
    y_send_now(3)

    zero_margins(a_src)
    for ref in (s_a, s_b, a_a, a_b):
        zero_margins(ref)
    zero_rows(a_src, (1, 2, 3, 12, 13, 14))
    zero_rows(a_a, (0, 1, 2, 3, 12, 13, 14, 15))
    zero_rows(a_b, (1, 2, 13, 14))

    width = margin[0, 0]
    column = lax.broadcasted_iota(jnp.int32, (BOX_NY, LANES), 0) + (BOX_Y - Y0)
    place = column + n * CY
    in_y = (column >= -width) & (column < CY + width) & (place >= 0) & (place < N * CY)

    def y_arrived(message, d):
        y_copy(message, 1 - d).wait_recv()

    for d, h in both:
        x_copy(PEN, d, h).wait_recv()
    for message in (0, 1, 2):
        each_side(lambda d, message=message: y_arrived(message, d))

    def unpack_penalty(d):
        unpack(pen, py_in.at[d], X0, CX, pen_comps, outer[d])
        unpack(pen, pc_in.at[d, 0], 1, OV, pen_comps, outer[d], base=7)
        unpack(pen, pc_in.at[d, 1], 12, OV, pen_comps, outer[d])

    each_side(unpack_penalty)

    def set_gain(i, carry):
        line = jnp.zeros((BOX_NY, LANES), jnp.int32) + (i - X0)
        inside = in_y & (line >= -width) & (line < CX + width)
        for h in (0, 1):
            value = DAMPING / (8.0 + pen[h, i, pl.ds(BOX_Y, BOX_NY), :])
            gain[h, i, pl.ds(BOX_Y, BOX_NY), :] = jnp.where(inside, value, 0.0)
        return carry

    lax.fori_loop(1, XR - 1, set_gain, 0)

    reduce_start(0, 1, reduce_finish(0, 0, jnp.add))

    def adjoint_first(i, carry):
        for h in (0, 1):
            g = gain[h, i, pl.ds(Y0, CY), :]
            for c in range(3):
                a_a[h, c, i, pl.ds(Y0, CY), :] = g * a_src[h, c, i, pl.ds(Y0, CY), :]
        return carry

    lax.fori_loop(X0, X0 + CX, adjoint_first, 0)
    sweep(a_a, a_b, a_src, gain, 3, 12)
    sweep(a_b, a_a, a_src, gain, 2, 13)
    for lo, hi in ((1, 3), (12, 14)):
        sweep(a_a, a_b, a_src, gain, lo, hi)
    for d, h in both:
        adjoint_copy(d, h).start()
    each_side(lambda d: pack(a_b, ac_out, 1, OV, all_comps, d, outer))
    each_side(lambda d: pack(a_b, ac_out, 12, OV, all_comps, d, outer, base=32))
    y_send_now(6)
    y_send_now(7)
    sweep(a_a, a_b, a_src, gain, 4, 11)
    each_side(lambda d: pack(a_b, ay_out, X0, CX, all_comps, d, outer))
    y_send_now(5)

    for d, h in both:
        x_copy(STATE, d, h).wait_recv()
    each_side(lambda d: pack(s_src, sc_out, 1, OV, all_comps, d, inner))
    each_side(lambda d: pack(s_src, sc_out, 12, OV, all_comps, d, inner, base=27))
    y_send_now(4)

    each_side(lambda d: y_arrived(3, d))
    each_side(lambda d: unpack(s_src, sy_in.at[d], X0, CX, all_comps, outer[d]))
    each_side(lambda d: y_arrived(4, d))

    def unpack_corners(d):
        unpack(s_src, sc_in.at[d], 1, OV, all_comps, outer[d])
        unpack(s_src, sc_in.at[d], 12, OV, all_comps, outer[d], base=27)

    each_side(unpack_corners)

    def state_first(i, carry):
        for h in (0, 1):
            g = gain[h, i, pl.ds(BOX_Y, BOX_NY), :]
            for c in range(3):
                s_a[h, c, i, pl.ds(BOX_Y, BOX_NY), :] = g * s_src[h, c, i, pl.ds(BOX_Y, BOX_NY), :]
        return carry

    lax.fori_loop(1, XR - 1, state_first, 0)
    sweep(s_a, s_b, s_src, gain, 2, 13)
    sweep(s_b, s_a, s_src, gain, 3, 12)
    sweep(s_a, s_b, s_src, gain, 4, 11, Y0, CY)

    coarse = reduce_finish(0, 1, jnp.add)
    inv = inverse[...]
    across = lax.broadcasted_iota(jnp.int32, (GROUPS, GROUPS), 1)
    along = lax.broadcasted_iota(jnp.int32, (GROUPS, GROUPS), 0)
    rhs = coarse[:, :GROUPS]
    state_row = jnp.sum(
        ((along.astype(F32) == own_group).astype(F32) - 1.0 / GROUPS) * inv, axis=0, keepdims=True
    )
    adjoint_column = jnp.sum(
        (across.astype(F32) == own_group).astype(F32) * inv, axis=1, keepdims=True
    )
    adjoint_row = jnp.sum(jnp.where(along == across, adjoint_column, 0.0), axis=0, keepdims=True)
    centred = rhs - jnp.sum(rhs, axis=1, keepdims=True) * (1.0 / GROUPS)
    by_state = jnp.sum(rhs * state_row, axis=1, keepdims=True)
    by_adjoint = jnp.sum(centred * adjoint_row, axis=1, keepdims=True)
    corr[...] = jnp.where(row < 3, by_state, by_adjoint)

    for message in (5, 6, 7):
        each_side(lambda d, message=message: y_arrived(message, d))

    def add_from_side(d):
        unpack(a_b, ay_in.at[d], X0, CX, all_comps, inner[d], add=True)
        unpack(a_b, ac_in.at[d, 0], X0, OV, all_comps, inner[d], add=True)
        unpack(a_b, ac_in.at[d, 1], X0 + CX - OV, OV, all_comps, inner[d], add=True)

    each_side(add_from_side)
    for d, h in both:
        adjoint_copy(d, h).wait_recv()

    def add_shares(k, carry):
        for h in (0, 1):
            for c in range(3):
                for d, x in ((0, X0), (1, X0 + CX - OV)):
                    a_b[h, c, x + k, pl.ds(Y0, CY), :] = (
                        a_b[h, c, x + k, pl.ds(Y0, CY), :] + ax_in[d, h, c, k]
                    )
        return carry

    for d, h in both:
        adjoint_copy(d, h).wait_send()
    lax.fori_loop(0, OV, add_shares, 0)

    def finish(i, peak):
        for h in (0, 1):
            z = slice(h * LANES, (h + 1) * LANES)
            raw = None
            for c in range(3):
                s = s_b[h, c, X0 + i, pl.ds(Y0, CY), :] + corr[pl.ds(c, 1), :]
                a = a_b[h, c, X0 + i, pl.ds(Y0, CY), :] + corr[pl.ds(c + 3, 1), :]
                state_out[c, i, :, z] = s
                adjoint_out[c, i, :, z] = a
                raw = s * a if raw is None else raw + s * a
            sens_out[i, :, z] = -raw
            size = jnp.abs(raw)
            peak = jnp.maximum(
                peak,
                jnp.maximum(jnp.maximum(size[0:8], size[8:16]), jnp.maximum(size[16:24], size[24:32])),
            )
        return peak

    peak = lax.fori_loop(0, CX, finish, jnp.zeros((8, LANES), F32))
    peak = jnp.max(peak, axis=0, keepdims=True)
    for s in (0, 1):
        reduce_start(1, s, peak)
        peak = reduce_finish(1, s, jnp.maximum)
    scale = 1.0 / (jnp.max(peak, axis=(0, 1), keepdims=True) + PEAK_EPS)

    def normalise(i, carry):
        sens_out[i] = sens_out[i] * scale
        return carry

    lax.fori_loop(0, CX, normalise, 0)

    for which in (PEN, STATE):
        for d, h in both:
            x_copy(which, d, h).wait_send()
    for message in range(8):
        each_side(lambda d, message=message: y_copy(message, d).wait_send())
    for use in (0, 1):
        for s in (0, 1):
            for k in range(1, len(stages[s]) + 1):
                reduce_copy(use, s, k).wait_send()


def write_out(state, adjoint, sens, state_out, adjoint_out, sens_out, sem):
    copies = [
        pltpu.make_async_copy(ref, out, sem.at[k])
        for k, (ref, out) in enumerate(
            ((state, state_out), (adjoint, adjoint_out), (sens, sens_out))
        )
    ]
    for copy in copies:
        copy.start()
    for copy in copies:
        copy.wait()


def body(state_rhs, adjoint_rhs, penalty, margin_width, owner_map, coarse_inv):
    vmem = pltpu.VMEM
    field = vmem((2, 3, XR, YR, LANES), F32)
    flat = vmem((2, XR, YR, LANES), F32)

    def message(rows):
        return [vmem((2, 2, rows, LANES), F32)] * 2

    dma = pltpu.SemaphoreType.DMA
    results = pl.pallas_call(
        kernel,
        out_shape=(
            pltpu.VMEM(state_rhs.shape, F32),
            pltpu.VMEM(adjoint_rhs.shape, F32),
            pltpu.VMEM(penalty.shape, F32),
        ),
        in_specs=[pl.BlockSpec(memory_space=pl.ANY)] * 3
        + [pl.BlockSpec(memory_space=pltpu.SMEM)]
        + [pl.BlockSpec(memory_space=vmem)] * 2,
        out_specs=(pl.BlockSpec(memory_space=vmem),) * 3,
        scratch_shapes=[field] * 6
        + [flat] * 2
        + message(24)
        + [vmem((2, 2, 2, 16, LANES), F32)]
        + message(72)
        + message(56)
        + message(72)
        + [
            vmem((2, 2, 64, LANES), F32),
            vmem((2, 2, 2, 32, LANES), F32),
            vmem((2, 2, 3, OV, CY, LANES), F32),
            vmem((48, 8, LANES), F32),
            vmem((48, 1, LANES), F32),
            vmem((8, LANES), F32),
            dma((6,)),
            dma((12,)),
            dma((12,)),
            dma((16,)),
            dma((16,)),
            dma((96,)),
            dma((96,)),
        ],
        compiler_params=pltpu.CompilerParams(
            collective_id=0, has_side_effects=True, vmem_limit_bytes=56 * 1024 * 1024
        ),
        name="schwarz",
    )(
        pltpu.with_memory_space_constraint(state_rhs, pltpu.HBM),
        pltpu.with_memory_space_constraint(adjoint_rhs, pltpu.HBM),
        pltpu.with_memory_space_constraint(penalty, pltpu.HBM),
        margin_width,
        owner_map.T,
        coarse_inv,
    )
    return pl.pallas_call(
        write_out,
        out_shape=tuple(jax.ShapeDtypeStruct(r.shape, F32) for r in results),
        in_specs=[pl.BlockSpec(memory_space=vmem)] * 3,
        out_specs=(pl.BlockSpec(memory_space=pltpu.HBM),) * 3,
        scratch_shapes=[dma((3,))],
        compiler_params=pltpu.CompilerParams(vmem_limit_bytes=2 * 1024 * 1024),
        name="write_out",
    )(*results)


def solution(mesh):
    placed = (
        P(None, "wide", "narrow", None),
        P(None, "wide", "narrow", None),
        P("wide", "narrow", None),
        P("wide", "narrow"),
        P(),
        P(),
    )
    return jax.shard_map(
        body,
        mesh=mesh,
        in_specs=placed,
        out_specs=(
            P(None, "wide", "narrow", None),
            P(None, "wide", "narrow", None),
            P("wide", "narrow", None),
        ),
        check_vma=False,
    )
```

```python
import functools

import jax
import jax.numpy as jnp
from jax import lax
from jax.experimental import pallas as pl
from jax.experimental.pallas import tpu as pltpu
from jax.sharding import PartitionSpec as P

MESH = pl.DeviceIdType.MESH
F32 = jnp.float32

OV = 3
CX = 8
CY = 32
LANES = 128
GROUPS = 64
W = 128
N = 4
DAMPING = 0.7
PEAK_EPS = 1e-06

XR = 16
YR = 48
X0 = 4
Y0 = 8
BOX_Y = 5
BOX_NY = 40
PEN, STATE = 0, 1


def next_and_previous(plus, minus, lane):
    a0, a1 = pltpu.roll(plus[0], LANES - 1, 1), pltpu.roll(plus[1], LANES - 1, 1)
    b0, b1 = pltpu.roll(minus[0], 1, 1), pltpu.roll(minus[1], 1, 1)
    last, first = lane == LANES - 1, lane == 0
    return (
        jnp.where(last, a1, a0) + jnp.where(first, 0.0, b0),
        jnp.where(last, 0.0, a1) + jnp.where(first, b0, b1),
    )


def sweep(src, dst, source, gain, lo, hi, y0=BOX_Y, ny=BOX_NY):
    lane = lax.broadcasted_iota(jnp.int32, (ny, LANES), 1)

    def line(i, carry):
        centre, plus, minus, rest = [], [], [], []
        for h in (0, 1):

            def at(c, di=0, dy=0, h=h):
                return src[h, c, i + di, pl.ds(y0 + dy, ny), :]

            x0, x1, x2 = at(0), at(0, 1), at(0, -1)
            y_0, y1, y2 = at(1), at(1, 0, 1), at(1, 0, -1)
            z0 = at(2)
            xz = 0.25 * (at(2, 1) - at(2, -1))
            yz = 0.25 * (at(2, 0, 1) - at(2, 0, -1))
            zz = 0.25 * ((x1 - x2) + (y1 - y2))
            twice = z0 + z0
            centre.append((x0, y_0, z0))
            plus.append((x0 + xz, y_0 + yz, twice + zz))
            minus.append((x0 - xz, y_0 - yz, twice - zz))
            own_x, own_y = x1 + x2, y1 + y2
            rest.append(
                (
                    (own_x + own_x)
                    + (at(0, 0, 1) + at(0, 0, -1))
                    + 0.25 * ((at(1, 1, 1) - at(1, 1, -1)) - (at(1, -1, 1) - at(1, -1, -1))),
                    (own_y + own_y)
                    + (at(1, 1) + at(1, -1))
                    + 0.25 * ((at(0, 1, 1) - at(0, 1, -1)) - (at(0, -1, 1) - at(0, -1, -1))),
                    (at(2, 1) + at(2, -1)) + (at(2, 0, 1) + at(2, 0, -1)),
                )
            )
        for c in range(3):
            along = next_and_previous((plus[0][c], plus[1][c]), (minus[0][c], minus[1][c]), lane)
            for h in (0, 1):
                total = source[h, c, i, pl.ds(y0, ny), :] + (rest[h][c] + along[h])
                g = gain[h, i, pl.ds(y0, ny), :]
                dst[h, c, i, pl.ds(y0, ny), :] = 0.3 * centre[h][c] + g * total
        return carry

    lax.fori_loop(lo, hi + 1, line, 0)


def zero_rows(ref, rows):
    for i in rows:
        for h in (0, 1):
            for c in range(3):
                ref[h, c, i] = jnp.zeros((YR, LANES), F32)


def zero_margins(ref):
    def one(i, carry):
        for h in (0, 1):
            for y in (0, Y0 + CY):
                if len(ref.shape) == 4:
                    ref[h, i, pl.ds(y, 8), :] = jnp.zeros((8, LANES), F32)
                else:
                    for c in range(3):
                        ref[h, c, i, pl.ds(y, 8), :] = jnp.zeros((8, LANES), F32)
        return carry

    lax.fori_loop(0, XR, one, 0)


def kernel(
    state,
    adjoint,
    penalty,
    margin,
    owner,
    inverse,
    state_out,
    adjoint_out,
    sens_out,
    s_src,
    a_src,
    s_a,
    s_b,
    a_a,
    a_b,
    pen,
    gain,
    py_out,
    py_in,
    pc_in,
    sy_out,
    sy_in,
    sc_in,
    ay_out,
    ay_in,
    ac_out,
    ac_in,
    pr_out,
    pr_in,
    sr_out,
    sr_in,
    ar_out,
    ar_in,
    ax_in,
    total_red,
    peak_red,
    corr,
    load_sem,
    x_send,
    x_recv,
    y_send,
    y_recv,
    r_send,
    r_recv,
):
    w, n = lax.axis_index("wide"), lax.axis_index("narrow")
    py, px, pz = w // 16, lax.rem(w // 4, 4), lax.rem(w, 4)
    ph, pc = n // 2, lax.rem(n, 2)
    left, right = lax.rem(w + W - 1, W), lax.rem(w + 1, W)
    down, up = lax.rem(n + N - 1, N), lax.rem(n + 1, N)
    stages = (
        [
            (py * 16 + px * 4 + lax.rem(pz + k // 4, 4), lax.rem(ph + k // 2 % 2, 2) * 2 + lax.rem(pc + k % 2, 2))
            for k in range(1, 16)
        ],
        [(lax.rem(py + k // 4, 8) * 16 + lax.rem(px + k % 4, 4) * 4 + pz, n) for k in range(1, 32)],
    )
    has_down, has_up = n > 0, n < N - 1

    barrier = pltpu.get_barrier_semaphore()
    for device in [(left, n), (right, n)] + stages[0] + stages[1]:
        pl.semaphore_signal(barrier, inc=1, device_id=device, device_id_type=MESH)

    @pl.when(has_down)
    def _():
        for at in (left, w, right):
            pl.semaphore_signal(barrier, inc=1, device_id=(at, down), device_id_type=MESH)

    @pl.when(has_up)
    def _():
        for at in (left, w, right):
            pl.semaphore_signal(barrier, inc=1, device_id=(at, up), device_id_type=MESH)

    loads = []
    own_x, own_y = pl.ds(X0, CX), pl.ds(Y0, CY)
    for k in range(3):
        for h in (0, 1):
            z = pl.ds(h * LANES, LANES)
            ref, target = (
                (penalty.at[:, :, z], pen.at[h, own_x, own_y, :]),
                (adjoint.at[:, :, :, z], a_src.at[h, :, own_x, own_y, :]),
                (state.at[:, :, :, z], s_src.at[h, :, own_x, own_y, :]),
            )[k]
            copy = pltpu.make_async_copy(ref, target, load_sem.at[2 * k + h])
            copy.start()
            loads.append(copy)

    zero_margins(s_src)
    peers = 48 + 3 * (has_down.astype(jnp.int32) + has_up.astype(jnp.int32))
    pl.semaphore_wait(barrier, peers)

    def x_copy(which, d, h):
        rows, target = (pl.ds(0, OV), pl.ds(12, OV)) if d == 0 else (pl.ds(CX - OV, OV), pl.ds(1, OV))
        z, own_y = pl.ds(h * LANES, LANES), pl.ds(Y0, CY)
        if which == PEN:
            ref, to = penalty.at[rows, :, z], pen.at[h, target, own_y, :]
        else:
            ref, to = state.at[:, rows, :, z], s_src.at[h, :, target, own_y, :]
        return pltpu.make_async_remote_copy(
            src_ref=ref,
            dst_ref=to,
            send_sem=x_send.at[4 * which + 2 * d + h],
            recv_sem=x_recv.at[4 * which + 2 * (1 - d) + h],
            device_id=(left if d == 0 else right, n),
            device_id_type=MESH,
        )

    def adjoint_copy(d, h):
        rows = pl.ds(1, OV) if d == 0 else pl.ds(12, OV)
        return pltpu.make_async_remote_copy(
            src_ref=a_b.at[h, :, rows, pl.ds(Y0, CY), :],
            dst_ref=ax_in.at[1 - d, h],
            send_sem=x_send.at[8 + 2 * d + h],
            recv_sem=x_recv.at[8 + 2 * (1 - d) + h],
            device_id=(left if d == 0 else right, n),
            device_id_type=MESH,
        )

    both = [(d, h) for d in (0, 1) for h in (0, 1)]
    for d, h in both:
        x_copy(PEN, d, h).start()

    def y_copy(message, d):
        out, land, rows, side, _ = messages[message]
        return pltpu.make_async_remote_copy(
            src_ref=out.at[d, :, rows, :],
            dst_ref=land.at[1 - d, :, rows, :] if side == 0 else land.at[1 - d, 2 - side],
            send_sem=y_send.at[2 * message + d],
            recv_sem=y_recv.at[2 * message + 1 - d],
            device_id=((w, left, right)[side], down if d == 0 else up),
            device_id_type=MESH,
        )

    messages = (
        (py_out, py_in, pl.ds(0, 24), 0, 0),
        (py_out, pc_in, pl.ds(0, 16), 1, 1),
        (py_out, pc_in, pl.ds(8, 16), 2, 1),
        (sy_out, sy_in, pl.ds(0, 72), 0, 0),
        (sy_out, sc_in, pl.ds(0, 32), 1, 1),
        (sy_out, sc_in, pl.ds(40, 32), 2, 1),
        (ay_out, ay_in, pl.ds(0, 72), 0, 0),
        (ac_out, ac_in, pl.ds(0, 32), 1, 1),
        (ac_out, ac_in, pl.ds(32, 32), 2, 1),
        (pr_out, pr_in, pl.ds(0, 24), 0, 2),
        (sr_out, sr_in, pl.ds(0, 56), 0, 2),
        (ar_out, ar_in, pl.ds(0, 56), 0, 2),
    )

    def each_side(action):
        @pl.when(has_down)
        def _():
            action(0)

        @pl.when(has_up)
        def _():
            action(1)

    def off_chip(action):
        @pl.when(n == 2)
        def _():
            action(0)

        @pl.when(n == 1)
        def _():
            action(1)

    def on_chip(action):
        @pl.when(pc == 1)
        def _():
            action(0)

        @pl.when(pc == 0)
        def _():
            action(1)

    def sides(message):
        return {0: each_side, 1: off_chip, 2: on_chip}[messages[message][4]]

    def y_send_now(message):
        sides(message)(lambda d: y_copy(message, d).start())

    inner = (Y0, Y0 + CY - OV)
    outer = (Y0 - OV, Y0 + CY)

    def rows_of(ref, h, c, i, y):
        return ref.at[h, i, pl.ds(y, OV), :] if c is None else ref.at[h, c, i, pl.ds(y, OV), :]

    def pack(ref, out, start, count, comps, d, ys, base=0):
        def step(k, carry):
            for h in (0, 1):
                for j, c in enumerate(comps):
                    slot = pl.ds(base + (k * len(comps) + j) * OV, OV)
                    out[d, h, slot, :] = rows_of(ref, h, c, start + k, ys[d])[...]
            return carry

        lax.fori_loop(0, count, step, 0)

    def unpack(ref, land, start, count, comps, y, base=0, add=False):
        def step(k, carry):
            for h in (0, 1):
                for j, c in enumerate(comps):
                    slot = pl.ds(base + (k * len(comps) + j) * OV, OV)
                    cell = rows_of(ref, h, c, start + k, y)
                    cell[...] = cell[...] + land[h, slot, :] if add else land[h, slot, :]
            return carry

        lax.fori_loop(0, count, step, 0)

    pen_comps, all_comps = (None,), (0, 1, 2)

    def reduce_copy(use, s, k):
        buffer, base = (total_red, peak_red)[use], 16 * s
        slot = 48 * use + base
        return pltpu.make_async_remote_copy(
            src_ref=buffer.at[base],
            dst_ref=buffer.at[base + k],
            send_sem=r_send.at[slot + k],
            recv_sem=r_recv.at[slot + k],
            device_id=stages[s][k - 1],
            device_id_type=MESH,
        )

    def reduce_start(use, s, value):
        (total_red, peak_red)[use][16 * s] = value
        for k in range(1, len(stages[s]) + 1):
            reduce_copy(use, s, k).start()

    def reduce_finish(use, s, combine):
        for k in range(1, len(stages[s]) + 1):
            reduce_copy(use, s, k).wait_recv()
        value = [(total_red, peak_red)[use][16 * s + k] for k in range(len(stages[s]) + 1)]
        while len(value) > 1:
            value = [combine(value[2 * k], value[2 * k + 1]) for k in range(len(value) // 2)]
        return value[0]

    for copy in loads[:2]:
        copy.wait()
    each_side(lambda d: pack(pen, py_out, X0, CX, pen_comps, d, inner))
    for message in (0, 1, 2):
        y_send_now(message)
    for copy in loads[2:]:
        copy.wait()

    spot = (lax.broadcasted_iota(jnp.int32, (N, W), 0) == n) & (
        lax.broadcasted_iota(jnp.int32, (N, W), 1) == w
    )
    own_group = jnp.sum(jnp.where(spot, owner[...].astype(F32), 0.0), axis=(0, 1), keepdims=True)
    pick = (lax.broadcasted_iota(jnp.int32, (1, LANES), 1).astype(F32) == own_group).astype(F32)
    row = lax.broadcasted_iota(jnp.int32, (8, LANES), 0)
    sums = jnp.zeros((8, LANES), F32)
    for k, ref in enumerate((s_src, a_src)):
        for c in range(3):

            def add(i, total, ref=ref, c=c):
                cells = ref[0, c, i, pl.ds(Y0, CY), :] + ref[1, c, i, pl.ds(Y0, CY), :]
                return total + ((cells[0:8] + cells[8:16]) + (cells[16:24] + cells[24:32]))

            total = lax.fori_loop(X0, X0 + CX, add, jnp.zeros((8, LANES), F32))
            mean = jnp.sum(total, axis=(0, 1), keepdims=True) * (1.0 / (CX * CY * 2 * LANES))
            sums = sums + jnp.where(row == 3 * k + c, mean * pick, 0.0)
    reduce_start(0, 0, sums)

    each_side(lambda d: pack(s_src, sy_out, X0, CX, all_comps, d, inner))
    for message in (3, 4, 5):
        y_send_now(message)
    for d, h in both:
        x_copy(STATE, d, h).start()

    zero_margins(a_src)
    for ref in (s_a, s_b, a_a, a_b):
        zero_margins(ref)
    zero_rows(a_src, (1, 2, 3, 12, 13, 14))
    zero_rows(a_a, (0, 1, 2, 3, 12, 13, 14, 15))
    zero_rows(a_b, (1, 2, 13, 14))

    width = margin[0, 0]
    column = lax.broadcasted_iota(jnp.int32, (BOX_NY, LANES), 0) + (BOX_Y - Y0)
    place = column + n * CY
    in_y = (column >= -width) & (column < CY + width) & (place >= 0) & (place < N * CY)

    def y_arrived(message, d):
        y_copy(message, 1 - d).wait_recv()

    for d, h in both:
        x_copy(PEN, d, h).wait_recv()
    on_chip(lambda d: pack(pen, pr_out, 1, OV, pen_comps, d, inner))
    on_chip(lambda d: pack(pen, pr_out, 12, OV, pen_comps, d, inner, base=9))
    y_send_now(9)
    for message in (0, 1, 2):
        sides(message)(lambda d, message=message: y_arrived(message, d))
    each_side(lambda d: unpack(pen, py_in.at[d], X0, CX, pen_comps, outer[d]))

    def unpack_penalty(d):
        unpack(pen, pc_in.at[d, 0], 1, OV, pen_comps, outer[d], base=7)
        unpack(pen, pc_in.at[d, 1], 12, OV, pen_comps, outer[d])

    off_chip(unpack_penalty)

    def unpack_relayed_penalty(d):
        y_arrived(9, d)
        unpack(pen, pr_in.at[d], 1, OV, pen_comps, outer[d])
        unpack(pen, pr_in.at[d], 12, OV, pen_comps, outer[d], base=9)

    on_chip(unpack_relayed_penalty)

    def set_gain(i, carry):
        line = jnp.zeros((BOX_NY, LANES), jnp.int32) + (i - X0)
        inside = in_y & (line >= -width) & (line < CX + width)
        for h in (0, 1):
            value = DAMPING / (8.0 + pen[h, i, pl.ds(BOX_Y, BOX_NY), :])
            gain[h, i, pl.ds(BOX_Y, BOX_NY), :] = jnp.where(inside, value, 0.0)
        return carry

    lax.fori_loop(1, XR - 1, set_gain, 0)

    reduce_start(0, 1, reduce_finish(0, 0, jnp.add))

    def adjoint_first(i, carry):
        for h in (0, 1):
            g = gain[h, i, pl.ds(Y0, CY), :]
            for c in range(3):
                a_a[h, c, i, pl.ds(Y0, CY), :] = g * a_src[h, c, i, pl.ds(Y0, CY), :]
        return carry

    lax.fori_loop(X0, X0 + CX, adjoint_first, 0)
    sweep(a_a, a_b, a_src, gain, 3, 12)
    sweep(a_b, a_a, a_src, gain, 2, 13)
    sweep(a_a, a_b, a_src, gain, 1, 14)
    each_side(lambda d: pack(a_b, ay_out, X0, CX, all_comps, d, outer))
    off_chip(lambda d: pack(a_b, ac_out, 1, OV, all_comps, d, outer))
    off_chip(lambda d: pack(a_b, ac_out, 12, OV, all_comps, d, outer, base=32))
    on_chip(lambda d: pack(a_b, ar_out, 1, OV, all_comps, d, outer))
    on_chip(lambda d: pack(a_b, ar_out, 12, OV, all_comps, d, outer, base=27))
    for message in (11, 6, 7, 8):
        y_send_now(message)

    def add_relayed(d):
        y_arrived(11, d)
        unpack(a_b, ar_in.at[d], 1, OV, all_comps, inner[d], add=True)
        unpack(a_b, ar_in.at[d], 12, OV, all_comps, inner[d], base=27, add=True)

    on_chip(add_relayed)
    for d, h in both:
        adjoint_copy(d, h).start()

    for d, h in both:
        x_copy(STATE, d, h).wait_recv()
    on_chip(lambda d: pack(s_src, sr_out, 1, OV, all_comps, d, inner))
    on_chip(lambda d: pack(s_src, sr_out, 12, OV, all_comps, d, inner, base=27))
    y_send_now(10)
    for message in (3, 4, 5):
        sides(message)(lambda d, message=message: y_arrived(message, d))
    each_side(lambda d: unpack(s_src, sy_in.at[d], X0, CX, all_comps, outer[d]))

    def unpack_state(d):
        unpack(s_src, sc_in.at[d, 0], 1, OV, all_comps, outer[d], base=5)
        unpack(s_src, sc_in.at[d, 1], 12, OV, all_comps, outer[d])

    off_chip(unpack_state)

    def unpack_relayed_state(d):
        y_arrived(10, d)
        unpack(s_src, sr_in.at[d], 1, OV, all_comps, outer[d])
        unpack(s_src, sr_in.at[d], 12, OV, all_comps, outer[d], base=27)

    on_chip(unpack_relayed_state)

    def state_first(i, carry):
        for h in (0, 1):
            g = gain[h, i, pl.ds(BOX_Y, BOX_NY), :]
            for c in range(3):
                s_a[h, c, i, pl.ds(BOX_Y, BOX_NY), :] = g * s_src[h, c, i, pl.ds(BOX_Y, BOX_NY), :]
        return carry

    lax.fori_loop(1, XR - 1, state_first, 0)
    sweep(s_a, s_b, s_src, gain, 2, 13)
    sweep(s_b, s_a, s_src, gain, 3, 12)
    sweep(s_a, s_b, s_src, gain, 4, 11, Y0, CY)

    coarse = reduce_finish(0, 1, jnp.add)
    inv = inverse[...]
    across = lax.broadcasted_iota(jnp.int32, (GROUPS, GROUPS), 1)
    along = lax.broadcasted_iota(jnp.int32, (GROUPS, GROUPS), 0)
    rhs = coarse[:, :GROUPS]
    state_row = jnp.sum(
        ((along.astype(F32) == own_group).astype(F32) - 1.0 / GROUPS) * inv, axis=0, keepdims=True
    )
    adjoint_column = jnp.sum(
        (across.astype(F32) == own_group).astype(F32) * inv, axis=1, keepdims=True
    )
    adjoint_row = jnp.sum(jnp.where(along == across, adjoint_column, 0.0), axis=0, keepdims=True)
    centred = rhs - jnp.sum(rhs, axis=1, keepdims=True) * (1.0 / GROUPS)
    by_state = jnp.sum(rhs * state_row, axis=1, keepdims=True)
    by_adjoint = jnp.sum(centred * adjoint_row, axis=1, keepdims=True)
    corr[...] = jnp.where(row < 3, by_state, by_adjoint)

    for message in (6, 7, 8):
        sides(message)(lambda d, message=message: y_arrived(message, d))
    each_side(lambda d: unpack(a_b, ay_in.at[d], X0, CX, all_comps, inner[d], add=True))

    def add_from_side(d):
        unpack(a_b, ac_in.at[d, 0], X0, OV, all_comps, inner[d], add=True)
        unpack(a_b, ac_in.at[d, 1], X0 + CX - OV, OV, all_comps, inner[d], add=True)

    off_chip(add_from_side)
    for d, h in both:
        adjoint_copy(d, h).wait_recv()

    def add_shares(k, carry):
        for h in (0, 1):
            for c in range(3):
                for d, x in ((0, X0), (1, X0 + CX - OV)):
                    a_b[h, c, x + k, pl.ds(Y0, CY), :] = (
                        a_b[h, c, x + k, pl.ds(Y0, CY), :] + ax_in[d, h, c, k]
                    )
        return carry

    for d, h in both:
        adjoint_copy(d, h).wait_send()
    lax.fori_loop(0, OV, add_shares, 0)

    def finish(i, peak):
        for h in (0, 1):
            z = slice(h * LANES, (h + 1) * LANES)
            raw = None
            for c in range(3):
                s = s_b[h, c, X0 + i, pl.ds(Y0, CY), :] + corr[pl.ds(c, 1), :]
                a = a_b[h, c, X0 + i, pl.ds(Y0, CY), :] + corr[pl.ds(c + 3, 1), :]
                state_out[c, i, :, z] = s
                adjoint_out[c, i, :, z] = a
                raw = s * a if raw is None else raw + s * a
            sens_out[i, :, z] = -raw
            size = jnp.abs(raw)
            peak = jnp.maximum(
                peak,
                jnp.maximum(jnp.maximum(size[0:8], size[8:16]), jnp.maximum(size[16:24], size[24:32])),
            )
        return peak

    peak = lax.fori_loop(0, CX, finish, jnp.zeros((8, LANES), F32))
    peak = jnp.max(peak, axis=0, keepdims=True)
    for s in (0, 1):
        reduce_start(1, s, peak)
        peak = reduce_finish(1, s, jnp.maximum)
    scale = 1.0 / (jnp.max(peak, axis=(0, 1), keepdims=True) + PEAK_EPS)

    def normalise(i, carry):
        sens_out[i] = sens_out[i] * scale
        return carry

    lax.fori_loop(0, CX, normalise, 0)

    for which in (PEN, STATE):
        for d, h in both:
            x_copy(which, d, h).wait_send()
    for message in range(len(messages)):
        sides(message)(lambda d, message=message: y_copy(message, d).wait_send())
    for use in (0, 1):
        for s in (0, 1):
            for k in range(1, len(stages[s]) + 1):
                reduce_copy(use, s, k).wait_send()


def write_out(state, adjoint, sens, state_out, adjoint_out, sens_out, sem):
    copies = [
        pltpu.make_async_copy(ref, out, sem.at[k])
        for k, (ref, out) in enumerate(
            ((state, state_out), (adjoint, adjoint_out), (sens, sens_out))
        )
    ]
    for copy in copies:
        copy.start()
    for copy in copies:
        copy.wait()


def body(state_rhs, adjoint_rhs, penalty, margin_width, owner_map, coarse_inv):
    vmem = pltpu.VMEM
    field = vmem((2, 3, XR, YR, LANES), F32)
    flat = vmem((2, XR, YR, LANES), F32)

    def message(rows):
        return [vmem((2, 2, rows, LANES), F32)] * 2

    dma = pltpu.SemaphoreType.DMA
    results = pl.pallas_call(
        kernel,
        out_shape=(
            pltpu.VMEM(state_rhs.shape, F32),
            pltpu.VMEM(adjoint_rhs.shape, F32),
            pltpu.VMEM(penalty.shape, F32),
        ),
        in_specs=[pl.BlockSpec(memory_space=pl.ANY)] * 3
        + [pl.BlockSpec(memory_space=pltpu.SMEM)]
        + [pl.BlockSpec(memory_space=vmem)] * 2,
        out_specs=(pl.BlockSpec(memory_space=vmem),) * 3,
        scratch_shapes=[field] * 6
        + [flat] * 2
        + message(24)
        + [vmem((2, 2, 2, 16, LANES), F32)]
        + message(72)
        + [vmem((2, 2, 2, 32, LANES), F32)]
        + message(72)
        + [
            vmem((2, 2, 64, LANES), F32),
            vmem((2, 2, 2, 32, LANES), F32),
        ]
        + message(24)
        + message(56)
        + message(56)
        + [
            vmem((2, 2, 3, OV, CY, LANES), F32),
            vmem((48, 8, LANES), F32),
            vmem((48, 1, LANES), F32),
            vmem((8, LANES), F32),
            dma((6,)),
            dma((12,)),
            dma((12,)),
            dma((24,)),
            dma((24,)),
            dma((96,)),
            dma((96,)),
        ],
        compiler_params=pltpu.CompilerParams(
            collective_id=0, has_side_effects=True, vmem_limit_bytes=56 * 1024 * 1024
        ),
        name="schwarz",
    )(
        pltpu.with_memory_space_constraint(state_rhs, pltpu.HBM),
        pltpu.with_memory_space_constraint(adjoint_rhs, pltpu.HBM),
        pltpu.with_memory_space_constraint(penalty, pltpu.HBM),
        margin_width,
        owner_map.T,
        coarse_inv,
    )
    return pl.pallas_call(
        write_out,
        out_shape=tuple(jax.ShapeDtypeStruct(r.shape, F32) for r in results),
        in_specs=[pl.BlockSpec(memory_space=vmem)] * 3,
        out_specs=(pl.BlockSpec(memory_space=pltpu.HBM),) * 3,
        scratch_shapes=[dma((3,))],
        compiler_params=pltpu.CompilerParams(vmem_limit_bytes=2 * 1024 * 1024),
        name="write_out",
    )(*results)


def solution(mesh):
    placed = (
        P(None, "wide", "narrow", None),
        P(None, "wide", "narrow", None),
        P("wide", "narrow", None),
        P("wide", "narrow"),
        P(),
        P(),
    )
    return jax.shard_map(
        body,
        mesh=mesh,
        in_specs=placed,
        out_specs=(
            P(None, "wide", "narrow", None),
            P(None, "wide", "narrow", None),
            P("wide", "narrow", None),
        ),
        check_vma=False,
    )
```

```python
import functools

import jax
import jax.numpy as jnp
from jax import lax
from jax.experimental import pallas as pl
from jax.experimental.pallas import tpu as pltpu
from jax.sharding import PartitionSpec as P

MESH = pl.DeviceIdType.MESH
F32 = jnp.float32

OV = 3
CX = 8
CY = 32
LANES = 128
GROUPS = 64
W = 128
N = 4
DAMPING = 0.7
PEAK_EPS = 1e-06

XR = 16
YR = 48
X0 = 4
Y0 = 8
BOX_Y = 5
BOX_NY = 40
PEN, STATE = 0, 1


def next_and_previous(plus, minus, lane):
    a0, a1 = pltpu.roll(plus[0], LANES - 1, 1), pltpu.roll(plus[1], LANES - 1, 1)
    b0, b1 = pltpu.roll(minus[0], 1, 1), pltpu.roll(minus[1], 1, 1)
    last, first = lane == LANES - 1, lane == 0
    return (
        jnp.where(last, a1, a0) + jnp.where(first, 0.0, b0),
        jnp.where(last, 0.0, a1) + jnp.where(first, b0, b1),
    )


def sweep(src, dst, source, gain, lo, hi, y0=BOX_Y, ny=BOX_NY):
    lane = lax.broadcasted_iota(jnp.int32, (ny, LANES), 1)

    def line(i, carry):
        centre, plus, minus, rest = [], [], [], []
        for h in (0, 1):

            def at(c, di=0, dy=0, h=h):
                return src[h, c, i + di, pl.ds(y0 + dy, ny), :]

            x0, x1, x2 = at(0), at(0, 1), at(0, -1)
            y_0, y1, y2 = at(1), at(1, 0, 1), at(1, 0, -1)
            z0 = at(2)
            xz = 0.25 * (at(2, 1) - at(2, -1))
            yz = 0.25 * (at(2, 0, 1) - at(2, 0, -1))
            zz = 0.25 * ((x1 - x2) + (y1 - y2))
            twice = z0 + z0
            centre.append((x0, y_0, z0))
            plus.append((x0 + xz, y_0 + yz, twice + zz))
            minus.append((x0 - xz, y_0 - yz, twice - zz))
            own_x, own_y = x1 + x2, y1 + y2
            rest.append(
                (
                    (own_x + own_x)
                    + (at(0, 0, 1) + at(0, 0, -1))
                    + 0.25 * ((at(1, 1, 1) - at(1, 1, -1)) - (at(1, -1, 1) - at(1, -1, -1))),
                    (own_y + own_y)
                    + (at(1, 1) + at(1, -1))
                    + 0.25 * ((at(0, 1, 1) - at(0, 1, -1)) - (at(0, -1, 1) - at(0, -1, -1))),
                    (at(2, 1) + at(2, -1)) + (at(2, 0, 1) + at(2, 0, -1)),
                )
            )
        for c in range(3):
            along = next_and_previous((plus[0][c], plus[1][c]), (minus[0][c], minus[1][c]), lane)
            for h in (0, 1):
                total = source[h, c, i, pl.ds(y0, ny), :] + (rest[h][c] + along[h])
                g = gain[h, i, pl.ds(y0, ny), :]
                dst[h, c, i, pl.ds(y0, ny), :] = 0.3 * centre[h][c] + g * total
        return carry

    lax.fori_loop(lo, hi + 1, line, 0)


def zero_rows(ref, rows):
    for i in rows:
        for h in (0, 1):
            for c in range(3):
                ref[h, c, i] = jnp.zeros((YR, LANES), F32)


def zero_margins(ref):
    def one(i, carry):
        for h in (0, 1):
            for y in (0, Y0 + CY):
                if len(ref.shape) == 4:
                    ref[h, i, pl.ds(y, 8), :] = jnp.zeros((8, LANES), F32)
                else:
                    for c in range(3):
                        ref[h, c, i, pl.ds(y, 8), :] = jnp.zeros((8, LANES), F32)
        return carry

    lax.fori_loop(0, XR, one, 0)


def kernel(
    state,
    adjoint,
    penalty,
    margin,
    owner,
    inverse,
    state_out,
    adjoint_out,
    sens_out,
    s_src,
    a_src,
    s_a,
    s_b,
    a_a,
    a_b,
    pen,
    gain,
    py_out,
    py_in,
    pc_in,
    sy_out,
    sy_in,
    sc_in,
    ay_out,
    ay_in,
    ac_out,
    ac_in,
    pr_out,
    pr_in,
    sr_out,
    sr_in,
    ar_out,
    ar_in,
    ax_in,
    total_red,
    peak_red,
    corr,
    load_sem,
    x_send,
    x_recv,
    y_send,
    y_recv,
    r_send,
    r_recv,
):
    w, n = lax.axis_index("wide"), lax.axis_index("narrow")
    py, px, pz = w // 16, lax.rem(w // 4, 4), lax.rem(w, 4)
    ph, pc = n // 2, lax.rem(n, 2)
    left, right = lax.rem(w + W - 1, W), lax.rem(w + 1, W)
    down, up = lax.rem(n + N - 1, N), lax.rem(n + 1, N)
    stages = (
        [
            (py * 16 + px * 4 + lax.rem(pz + k // 4, 4), lax.rem(ph + k // 2 % 2, 2) * 2 + lax.rem(pc + k % 2, 2))
            for k in range(1, 16)
        ],
        [(lax.rem(py + k // 4, 8) * 16 + lax.rem(px + k % 4, 4) * 4 + pz, n) for k in range(1, 32)],
    )
    has_down, has_up = n > 0, n < N - 1

    barrier = pltpu.get_barrier_semaphore()
    for device in [(left, n), (right, n)] + stages[0] + stages[1]:
        pl.semaphore_signal(barrier, inc=1, device_id=device, device_id_type=MESH)

    @pl.when(has_down)
    def _():
        for at in (left, w, right):
            pl.semaphore_signal(barrier, inc=1, device_id=(at, down), device_id_type=MESH)

    @pl.when(has_up)
    def _():
        for at in (left, w, right):
            pl.semaphore_signal(barrier, inc=1, device_id=(at, up), device_id_type=MESH)

    loads = []
    own_x, own_y = pl.ds(X0, CX), pl.ds(Y0, CY)
    for k in range(3):
        for h in (0, 1):
            z = pl.ds(h * LANES, LANES)
            ref, target = (
                (penalty.at[:, :, z], pen.at[h, own_x, own_y, :]),
                (adjoint.at[:, :, :, z], a_src.at[h, :, own_x, own_y, :]),
                (state.at[:, :, :, z], s_src.at[h, :, own_x, own_y, :]),
            )[k]
            copy = pltpu.make_async_copy(ref, target, load_sem.at[2 * k + h])
            copy.start()
            loads.append(copy)

    zero_margins(s_src)
    peers = 48 + 3 * (has_down.astype(jnp.int32) + has_up.astype(jnp.int32))
    pl.semaphore_wait(barrier, peers)

    def x_copy(which, d, h):
        rows, target = (pl.ds(0, OV), pl.ds(12, OV)) if d == 0 else (pl.ds(CX - OV, OV), pl.ds(1, OV))
        z, own_y = pl.ds(h * LANES, LANES), pl.ds(Y0, CY)
        if which == PEN:
            ref, to = penalty.at[rows, :, z], pen.at[h, target, own_y, :]
        else:
            ref, to = state.at[:, rows, :, z], s_src.at[h, :, target, own_y, :]
        return pltpu.make_async_remote_copy(
            src_ref=ref,
            dst_ref=to,
            send_sem=x_send.at[4 * which + 2 * d + h],
            recv_sem=x_recv.at[4 * which + 2 * (1 - d) + h],
            device_id=(left if d == 0 else right, n),
            device_id_type=MESH,
        )

    def adjoint_copy(d, h):
        rows = pl.ds(1, OV) if d == 0 else pl.ds(12, OV)
        return pltpu.make_async_remote_copy(
            src_ref=a_b.at[h, :, rows, pl.ds(Y0, CY), :],
            dst_ref=ax_in.at[1 - d, h],
            send_sem=x_send.at[8 + 2 * d + h],
            recv_sem=x_recv.at[8 + 2 * (1 - d) + h],
            device_id=(left if d == 0 else right, n),
            device_id_type=MESH,
        )

    both = [(d, h) for d in (0, 1) for h in (0, 1)]
    for d, h in both:
        x_copy(PEN, d, h).start()

    def y_copy(message, d):
        out, land, rows, side, _ = messages[message]
        return pltpu.make_async_remote_copy(
            src_ref=out.at[d, :, rows, :],
            dst_ref=land.at[1 - d, :, rows, :] if side == 0 else land.at[1 - d, 2 - side],
            send_sem=y_send.at[2 * message + d],
            recv_sem=y_recv.at[2 * message + 1 - d],
            device_id=((w, left, right)[side], down if d == 0 else up),
            device_id_type=MESH,
        )

    messages = (
        (py_out, py_in, pl.ds(0, 24), 0, 0),
        (py_out, pc_in, pl.ds(0, 16), 1, 1),
        (py_out, pc_in, pl.ds(8, 16), 2, 1),
        (sy_out, sy_in, pl.ds(0, 72), 0, 0),
        (sy_out, sc_in, pl.ds(0, 32), 1, 1),
        (sy_out, sc_in, pl.ds(40, 32), 2, 1),
        (ay_out, ay_in, pl.ds(0, 72), 0, 0),
        (ac_out, ac_in, pl.ds(0, 32), 1, 1),
        (ac_out, ac_in, pl.ds(32, 32), 2, 1),
        (pr_out, pr_in, pl.ds(0, 24), 0, 2),
        (sr_out, sr_in, pl.ds(0, 56), 0, 2),
        (ar_out, ar_in, pl.ds(0, 56), 0, 2),
    )

    def each_side(action):
        @pl.when(has_down)
        def _():
            action(0)

        @pl.when(has_up)
        def _():
            action(1)

    def off_chip(action):
        @pl.when(n == 2)
        def _():
            action(0)

        @pl.when(n == 1)
        def _():
            action(1)

    def on_chip(action):
        @pl.when(pc == 1)
        def _():
            action(0)

        @pl.when(pc == 0)
        def _():
            action(1)

    def sides(message):
        return {0: each_side, 1: off_chip, 2: on_chip}[messages[message][4]]

    def y_send_now(message):
        sides(message)(lambda d: y_copy(message, d).start())

    inner = (Y0, Y0 + CY - OV)
    outer = (Y0 - OV, Y0 + CY)

    def rows_of(ref, h, c, i, y):
        return ref.at[h, i, pl.ds(y, OV), :] if c is None else ref.at[h, c, i, pl.ds(y, OV), :]

    def pack(ref, out, start, count, comps, d, ys, base=0):
        def step(k, carry):
            for h in (0, 1):
                for j, c in enumerate(comps):
                    slot = pl.ds(base + (k * len(comps) + j) * OV, OV)
                    out[d, h, slot, :] = rows_of(ref, h, c, start + k, ys[d])[...]
            return carry

        lax.fori_loop(0, count, step, 0)

    def unpack(ref, land, start, count, comps, y, base=0, add=False):
        def step(k, carry):
            for h in (0, 1):
                for j, c in enumerate(comps):
                    slot = pl.ds(base + (k * len(comps) + j) * OV, OV)
                    cell = rows_of(ref, h, c, start + k, y)
                    cell[...] = cell[...] + land[h, slot, :] if add else land[h, slot, :]
            return carry

        lax.fori_loop(0, count, step, 0)

    pen_comps, all_comps = (None,), (0, 1, 2)

    def reduce_copy(use, s, k):
        buffer, base = (total_red, peak_red)[use], 16 * s
        return pltpu.make_async_remote_copy(
            src_ref=buffer.at[base],
            dst_ref=buffer.at[base + k],
            send_sem=r_send.at[2 * use + s],
            recv_sem=r_recv.at[2 * use + s],
            device_id=stages[s][k - 1],
            device_id_type=MESH,
        )

    def reduce_all(use, s):
        count = len(stages[s])
        slots = (total_red, peak_red)[use].at[pl.ds(16 * s + 1, count)]
        return pltpu.make_async_remote_copy(
            src_ref=slots,
            dst_ref=slots,
            send_sem=r_send.at[2 * use + s],
            recv_sem=r_recv.at[2 * use + s],
            device_id=stages[s][0],
            device_id_type=MESH,
        )

    def reduce_start(use, s, value):
        (total_red, peak_red)[use][16 * s] = value
        for k in range(1, len(stages[s]) + 1):
            reduce_copy(use, s, k).start()

    def reduce_finish(use, s, combine):
        reduce_all(use, s).wait_recv()
        value = [(total_red, peak_red)[use][16 * s + k] for k in range(len(stages[s]) + 1)]
        while len(value) > 1:
            value = [combine(value[2 * k], value[2 * k + 1]) for k in range(len(value) // 2)]
        return value[0]

    for copy in loads[:2]:
        copy.wait()
    each_side(lambda d: pack(pen, py_out, X0, CX, pen_comps, d, inner))
    for message in (0, 1, 2):
        y_send_now(message)
    for copy in loads[2:]:
        copy.wait()

    spot = (lax.broadcasted_iota(jnp.int32, (N, W), 0) == n) & (
        lax.broadcasted_iota(jnp.int32, (N, W), 1) == w
    )
    own_group = jnp.sum(jnp.where(spot, owner[...].astype(F32), 0.0), axis=(0, 1), keepdims=True)
    pick = (lax.broadcasted_iota(jnp.int32, (1, LANES), 1).astype(F32) == own_group).astype(F32)
    row = lax.broadcasted_iota(jnp.int32, (8, LANES), 0)
    sums = jnp.zeros((8, LANES), F32)
    for k, ref in enumerate((s_src, a_src)):
        for c in range(3):

            def add(i, total, ref=ref, c=c):
                cells = ref[0, c, i, pl.ds(Y0, CY), :] + ref[1, c, i, pl.ds(Y0, CY), :]
                return total + ((cells[0:8] + cells[8:16]) + (cells[16:24] + cells[24:32]))

            total = lax.fori_loop(X0, X0 + CX, add, jnp.zeros((8, LANES), F32))
            mean = jnp.sum(total, axis=(0, 1), keepdims=True) * (1.0 / (CX * CY * 2 * LANES))
            sums = sums + jnp.where(row == 3 * k + c, mean * pick, 0.0)
    reduce_start(0, 0, sums)

    each_side(lambda d: pack(s_src, sy_out, X0, CX, all_comps, d, inner))
    for message in (3, 4, 5):
        y_send_now(message)
    for d, h in both:
        x_copy(STATE, d, h).start()

    zero_margins(a_src)
    for ref in (s_a, s_b, a_a, a_b):
        zero_margins(ref)
    zero_rows(a_src, (1, 2, 3, 12, 13, 14))
    zero_rows(a_a, (0, 1, 2, 3, 12, 13, 14, 15))
    zero_rows(a_b, (1, 2, 13, 14))

    width = margin[0, 0]
    column = lax.broadcasted_iota(jnp.int32, (BOX_NY, LANES), 0) + (BOX_Y - Y0)
    place = column + n * CY
    in_y = (column >= -width) & (column < CY + width) & (place >= 0) & (place < N * CY)

    def y_arrived(message, d):
        y_copy(message, 1 - d).wait_recv()

    for d, h in both:
        x_copy(PEN, d, h).wait_recv()
    on_chip(lambda d: pack(pen, pr_out, 1, OV, pen_comps, d, inner))
    on_chip(lambda d: pack(pen, pr_out, 12, OV, pen_comps, d, inner, base=9))
    y_send_now(9)
    for message in (0, 1, 2):
        sides(message)(lambda d, message=message: y_arrived(message, d))
    each_side(lambda d: unpack(pen, py_in.at[d], X0, CX, pen_comps, outer[d]))

    def unpack_penalty(d):
        unpack(pen, pc_in.at[d, 0], 1, OV, pen_comps, outer[d], base=7)
        unpack(pen, pc_in.at[d, 1], 12, OV, pen_comps, outer[d])

    off_chip(unpack_penalty)

    def unpack_relayed_penalty(d):
        y_arrived(9, d)
        unpack(pen, pr_in.at[d], 1, OV, pen_comps, outer[d])
        unpack(pen, pr_in.at[d], 12, OV, pen_comps, outer[d], base=9)

    on_chip(unpack_relayed_penalty)

    def set_gain(i, carry):
        line = jnp.zeros((BOX_NY, LANES), jnp.int32) + (i - X0)
        inside = in_y & (line >= -width) & (line < CX + width)
        for h in (0, 1):
            value = DAMPING / (8.0 + pen[h, i, pl.ds(BOX_Y, BOX_NY), :])
            gain[h, i, pl.ds(BOX_Y, BOX_NY), :] = jnp.where(inside, value, 0.0)
        return carry

    lax.fori_loop(1, XR - 1, set_gain, 0)

    def adjoint_first(i, carry):
        for h in (0, 1):
            g = gain[h, i, pl.ds(Y0, CY), :]
            for c in range(3):
                a_a[h, c, i, pl.ds(Y0, CY), :] = g * a_src[h, c, i, pl.ds(Y0, CY), :]
        return carry

    lax.fori_loop(X0, X0 + CX, adjoint_first, 0)
    sweep(a_a, a_b, a_src, gain, 3, 12)
    sweep(a_b, a_a, a_src, gain, 2, 13)
    sweep(a_a, a_b, a_src, gain, 1, 14)
    each_side(lambda d: pack(a_b, ay_out, X0, CX, all_comps, d, outer))
    off_chip(lambda d: pack(a_b, ac_out, 1, OV, all_comps, d, outer))
    off_chip(lambda d: pack(a_b, ac_out, 12, OV, all_comps, d, outer, base=32))
    on_chip(lambda d: pack(a_b, ar_out, 1, OV, all_comps, d, outer))
    on_chip(lambda d: pack(a_b, ar_out, 12, OV, all_comps, d, outer, base=27))
    for message in (11, 6, 7, 8):
        y_send_now(message)

    def add_relayed(d):
        y_arrived(11, d)
        unpack(a_b, ar_in.at[d], 1, OV, all_comps, inner[d], add=True)
        unpack(a_b, ar_in.at[d], 12, OV, all_comps, inner[d], base=27, add=True)

    on_chip(add_relayed)
    for d, h in both:
        adjoint_copy(d, h).start()

    reduce_start(0, 1, reduce_finish(0, 0, jnp.add))

    for d, h in both:
        x_copy(STATE, d, h).wait_recv()
    on_chip(lambda d: pack(s_src, sr_out, 1, OV, all_comps, d, inner))
    on_chip(lambda d: pack(s_src, sr_out, 12, OV, all_comps, d, inner, base=27))
    y_send_now(10)
    for message in (3, 4, 5):
        sides(message)(lambda d, message=message: y_arrived(message, d))
    each_side(lambda d: unpack(s_src, sy_in.at[d], X0, CX, all_comps, outer[d]))

    def unpack_state(d):
        unpack(s_src, sc_in.at[d, 0], 1, OV, all_comps, outer[d], base=5)
        unpack(s_src, sc_in.at[d, 1], 12, OV, all_comps, outer[d])

    off_chip(unpack_state)

    def unpack_relayed_state(d):
        y_arrived(10, d)
        unpack(s_src, sr_in.at[d], 1, OV, all_comps, outer[d])
        unpack(s_src, sr_in.at[d], 12, OV, all_comps, outer[d], base=27)

    on_chip(unpack_relayed_state)

    def state_first(i, carry):
        for h in (0, 1):
            g = gain[h, i, pl.ds(BOX_Y, BOX_NY), :]
            for c in range(3):
                s_a[h, c, i, pl.ds(BOX_Y, BOX_NY), :] = g * s_src[h, c, i, pl.ds(BOX_Y, BOX_NY), :]
        return carry

    lax.fori_loop(1, XR - 1, state_first, 0)
    sweep(s_a, s_b, s_src, gain, 2, 13)
    sweep(s_b, s_a, s_src, gain, 3, 12)
    sweep(s_a, s_b, s_src, gain, 4, 11, Y0, CY)

    coarse = reduce_finish(0, 1, jnp.add)
    inv = inverse[...]
    across = lax.broadcasted_iota(jnp.int32, (GROUPS, GROUPS), 1)
    along = lax.broadcasted_iota(jnp.int32, (GROUPS, GROUPS), 0)
    rhs = coarse[:, :GROUPS]
    state_row = jnp.sum(
        ((along.astype(F32) == own_group).astype(F32) - 1.0 / GROUPS) * inv, axis=0, keepdims=True
    )
    adjoint_column = jnp.sum(
        (across.astype(F32) == own_group).astype(F32) * inv, axis=1, keepdims=True
    )
    adjoint_row = jnp.sum(jnp.where(along == across, adjoint_column, 0.0), axis=0, keepdims=True)
    centred = rhs - jnp.sum(rhs, axis=1, keepdims=True) * (1.0 / GROUPS)
    by_state = jnp.sum(rhs * state_row, axis=1, keepdims=True)
    by_adjoint = jnp.sum(centred * adjoint_row, axis=1, keepdims=True)
    corr[...] = jnp.where(row < 3, by_state, by_adjoint)

    for message in (6, 7, 8):
        sides(message)(lambda d, message=message: y_arrived(message, d))
    each_side(lambda d: unpack(a_b, ay_in.at[d], X0, CX, all_comps, inner[d], add=True))

    def add_from_side(d):
        unpack(a_b, ac_in.at[d, 0], X0, OV, all_comps, inner[d], add=True)
        unpack(a_b, ac_in.at[d, 1], X0 + CX - OV, OV, all_comps, inner[d], add=True)

    off_chip(add_from_side)

    def correct(i, carry):
        for h in (0, 1):
            z = slice(h * LANES, (h + 1) * LANES)
            for c in range(3):
                state_out[c, i, :, z] = s_b[h, c, X0 + i, pl.ds(Y0, CY), :] + corr[pl.ds(c, 1), :]
                adjoint_out[c, i, :, z] = a_b[h, c, X0 + i, pl.ds(Y0, CY), :] + corr[pl.ds(c + 3, 1), :]
        return carry

    lax.fori_loop(0, CX, correct, 0)

    def product(i, peak, share=None):
        for h in (0, 1):
            z = slice(h * LANES, (h + 1) * LANES)
            raw = None
            for c in range(3):
                a = adjoint_out[c, i, :, z]
                if share is not None:
                    a = a + share[h, c]
                    adjoint_out[c, i, :, z] = a
                s = state_out[c, i, :, z]
                raw = s * a if raw is None else raw + s * a
            sens_out[i, :, z] = -raw
            size = jnp.abs(raw)
            peak = jnp.maximum(
                peak,
                jnp.maximum(jnp.maximum(size[0:8], size[8:16]), jnp.maximum(size[16:24], size[24:32])),
            )
        return peak

    peak = lax.fori_loop(OV, CX - OV, product, jnp.zeros((8, LANES), F32))
    for d, base in ((0, 0), (1, CX - OV)):
        for h in (0, 1):
            adjoint_copy(1 - d, h).wait_recv()

        def with_share(k, peak, d=d, base=base):
            share = {(h, c): ax_in[d, h, c, k] for h in (0, 1) for c in range(3)}
            return product(base + k, peak, share)

        peak = lax.fori_loop(0, OV, with_share, peak)

    reduce_start(1, 0, jnp.max(peak, axis=0, keepdims=True))

    for which in (PEN, STATE):
        for d, h in both:
            x_copy(which, d, h).wait_send()
    for d, h in both:
        adjoint_copy(d, h).wait_send()
    for message in range(len(messages)):
        sides(message)(lambda d, message=message: y_copy(message, d).wait_send())
    for s in (0, 1):
        reduce_all(0, s).wait_send()

    reduce_start(1, 1, reduce_finish(1, 0, jnp.maximum))
    reduce_all(1, 0).wait_send()
    peak = reduce_finish(1, 1, jnp.maximum)
    scale = 1.0 / (jnp.max(peak, axis=1, keepdims=True) + PEAK_EPS)

    def normalise(i, carry):
        sens_out[i] = sens_out[i] * scale
        return carry

    lax.fori_loop(0, CX, normalise, 0)
    reduce_all(1, 1).wait_send()


def write_out(state, adjoint, sens, state_out, adjoint_out, sens_out, sem):
    copies = [
        pltpu.make_async_copy(ref, out, sem.at[k])
        for k, (ref, out) in enumerate(
            ((state, state_out), (adjoint, adjoint_out), (sens, sens_out))
        )
    ]
    for copy in copies:
        copy.start()
    for copy in copies:
        copy.wait()


def body(state_rhs, adjoint_rhs, penalty, margin_width, owner_map, coarse_inv):
    vmem = pltpu.VMEM
    field = vmem((2, 3, XR, YR, LANES), F32)
    flat = vmem((2, XR, YR, LANES), F32)

    def message(rows):
        return [vmem((2, 2, rows, LANES), F32)] * 2

    dma = pltpu.SemaphoreType.DMA
    results = pl.pallas_call(
        kernel,
        out_shape=(
            pltpu.VMEM(state_rhs.shape, F32),
            pltpu.VMEM(adjoint_rhs.shape, F32),
            pltpu.VMEM(penalty.shape, F32),
        ),
        in_specs=[pl.BlockSpec(memory_space=pl.ANY)] * 3
        + [pl.BlockSpec(memory_space=pltpu.SMEM)]
        + [pl.BlockSpec(memory_space=vmem)] * 2,
        out_specs=(pl.BlockSpec(memory_space=vmem),) * 3,
        scratch_shapes=[field] * 6
        + [flat] * 2
        + message(24)
        + [vmem((2, 2, 2, 16, LANES), F32)]
        + message(72)
        + [vmem((2, 2, 2, 32, LANES), F32)]
        + message(72)
        + [
            vmem((2, 2, 64, LANES), F32),
            vmem((2, 2, 2, 32, LANES), F32),
        ]
        + message(24)
        + message(56)
        + message(56)
        + [
            vmem((2, 2, 3, OV, CY, LANES), F32),
            vmem((48, 8, LANES), F32),
            vmem((48, 1, LANES), F32),
            vmem((8, LANES), F32),
            dma((6,)),
            dma((12,)),
            dma((12,)),
            dma((24,)),
            dma((24,)),
            dma((4,)),
            dma((4,)),
        ],
        compiler_params=pltpu.CompilerParams(
            collective_id=0, has_side_effects=True, vmem_limit_bytes=56 * 1024 * 1024
        ),
        name="schwarz",
    )(
        pltpu.with_memory_space_constraint(state_rhs, pltpu.HBM),
        pltpu.with_memory_space_constraint(adjoint_rhs, pltpu.HBM),
        pltpu.with_memory_space_constraint(penalty, pltpu.HBM),
        margin_width,
        owner_map.T,
        coarse_inv,
    )
    return pl.pallas_call(
        write_out,
        out_shape=tuple(jax.ShapeDtypeStruct(r.shape, F32) for r in results),
        in_specs=[pl.BlockSpec(memory_space=vmem)] * 3,
        out_specs=(pl.BlockSpec(memory_space=pltpu.HBM),) * 3,
        scratch_shapes=[dma((3,))],
        compiler_params=pltpu.CompilerParams(vmem_limit_bytes=2 * 1024 * 1024),
        name="write_out",
    )(*results)


def solution(mesh):
    placed = (
        P(None, "wide", "narrow", None),
        P(None, "wide", "narrow", None),
        P("wide", "narrow", None),
        P("wide", "narrow"),
        P(),
        P(),
    )
    return jax.shard_map(
        body,
        mesh=mesh,
        in_specs=placed,
        out_specs=(
            P(None, "wide", "narrow", None),
            P(None, "wide", "narrow", None),
            P("wide", "narrow", None),
        ),
        check_vma=False,
    )
```

```python
import functools

import jax
import jax.numpy as jnp
from jax import lax
from jax.experimental import pallas as pl
from jax.experimental.pallas import tpu as pltpu
from jax.sharding import PartitionSpec as P

MESH = pl.DeviceIdType.MESH
F32 = jnp.float32

OV = 3
CX = 8
CY = 32
LANES = 128
GROUPS = 64
W = 128
N = 4
DAMPING = 0.7
PEAK_EPS = 1e-06

XR = 16
YR = 48
X0 = 4
Y0 = 8
BOX_Y = 5
BOX_NY = 40
PEN, STATE, FIRST = 0, 1, 2


def next_and_previous(plus, minus, lane):
    a0, a1 = pltpu.roll(plus[0], LANES - 1, 1), pltpu.roll(plus[1], LANES - 1, 1)
    b0, b1 = pltpu.roll(minus[0], 1, 1), pltpu.roll(minus[1], 1, 1)
    last, first = lane == LANES - 1, lane == 0
    return (
        jnp.where(last, a1, a0) + jnp.where(first, 0.0, b0),
        jnp.where(last, 0.0, a1) + jnp.where(first, b0, b1),
    )


def sweep(src, dst, source, gain, lo, hi, y0=BOX_Y, ny=BOX_NY):
    lane = lax.broadcasted_iota(jnp.int32, (ny, LANES), 1)

    def line(i, carry):
        centre, plus, minus, rest = [], [], [], []
        for h in (0, 1):

            def at(c, di=0, dy=0, h=h):
                return src[h, c, i + di, pl.ds(y0 + dy, ny), :]

            x0, x1, x2 = at(0), at(0, 1), at(0, -1)
            y_0, y1, y2 = at(1), at(1, 0, 1), at(1, 0, -1)
            z0 = at(2)
            xz = 0.25 * (at(2, 1) - at(2, -1))
            yz = 0.25 * (at(2, 0, 1) - at(2, 0, -1))
            zz = 0.25 * ((x1 - x2) + (y1 - y2))
            twice = z0 + z0
            centre.append((x0, y_0, z0))
            plus.append((x0 + xz, y_0 + yz, twice + zz))
            minus.append((x0 - xz, y_0 - yz, twice - zz))
            own_x, own_y = x1 + x2, y1 + y2
            rest.append(
                (
                    (own_x + own_x)
                    + (at(0, 0, 1) + at(0, 0, -1))
                    + 0.25 * ((at(1, 1, 1) - at(1, 1, -1)) - (at(1, -1, 1) - at(1, -1, -1))),
                    (own_y + own_y)
                    + (at(1, 1) + at(1, -1))
                    + 0.25 * ((at(0, 1, 1) - at(0, 1, -1)) - (at(0, -1, 1) - at(0, -1, -1))),
                    (at(2, 1) + at(2, -1)) + (at(2, 0, 1) + at(2, 0, -1)),
                )
            )
        for c in range(3):
            along = next_and_previous((plus[0][c], plus[1][c]), (minus[0][c], minus[1][c]), lane)
            for h in (0, 1):
                total = source[h, c, i, pl.ds(y0, ny), :] + (rest[h][c] + along[h])
                g = gain[h, i, pl.ds(y0, ny), :]
                dst[h, c, i, pl.ds(y0, ny), :] = 0.3 * centre[h][c] + g * total
        return carry

    lax.fori_loop(lo, hi + 1, line, 0)


def zero_rows(ref, rows):
    for i in rows:
        for h in (0, 1):
            for c in range(3):
                ref[h, c, i] = jnp.zeros((YR, LANES), F32)


def zero_margins(ref):
    def one(i, carry):
        for h in (0, 1):
            for y in (0, Y0 + CY):
                if len(ref.shape) == 4:
                    ref[h, i, pl.ds(y, 8), :] = jnp.zeros((8, LANES), F32)
                else:
                    for c in range(3):
                        ref[h, c, i, pl.ds(y, 8), :] = jnp.zeros((8, LANES), F32)
        return carry

    lax.fori_loop(0, XR, one, 0)


def kernel(
    state,
    adjoint,
    penalty,
    margin,
    owner,
    inverse,
    state_out,
    adjoint_out,
    sens_out,
    s_src,
    a_src,
    s_a,
    s_b,
    a_a,
    a_b,
    pen,
    gain,
    py_out,
    py_in,
    pc_in,
    sy_out,
    sy_in,
    sc_in,
    ay_out,
    ay_in,
    ac_out,
    ac_in,
    pr_out,
    pr_in,
    sr_out,
    sr_in,
    ar_out,
    ar_in,
    ax_in,
    first_out,
    total_red,
    peak_red,
    corr,
    load_sem,
    x_send,
    x_recv,
    y_send,
    y_recv,
    r_send,
    r_recv,
):
    w, n = lax.axis_index("wide"), lax.axis_index("narrow")
    py, px, pz = w // 16, lax.rem(w // 4, 4), lax.rem(w, 4)
    ph, pc = n // 2, lax.rem(n, 2)
    left, right = lax.rem(w + W - 1, W), lax.rem(w + 1, W)
    down, up = lax.rem(n + N - 1, N), lax.rem(n + 1, N)
    stages = (
        [
            (py * 16 + px * 4 + lax.rem(pz + k // 4, 4), lax.rem(ph + k // 2 % 2, 2) * 2 + lax.rem(pc + k % 2, 2))
            for k in range(1, 16)
        ],
        [(lax.rem(py + k // 4, 8) * 16 + lax.rem(px + k % 4, 4) * 4 + pz, n) for k in range(1, 32)],
    )
    has_down, has_up = n > 0, n < N - 1

    barrier = pltpu.get_barrier_semaphore()
    for device in [(left, n), (right, n)] + stages[0] + stages[1]:
        pl.semaphore_signal(barrier, inc=1, device_id=device, device_id_type=MESH)

    @pl.when(has_down)
    def _():
        for at in (left, w, right):
            pl.semaphore_signal(barrier, inc=1, device_id=(at, down), device_id_type=MESH)

    @pl.when(has_up)
    def _():
        for at in (left, w, right):
            pl.semaphore_signal(barrier, inc=1, device_id=(at, up), device_id_type=MESH)

    loads = []
    own_x, own_y = pl.ds(X0, CX), pl.ds(Y0, CY)
    for k in range(3):
        for h in (0, 1):
            z = pl.ds(h * LANES, LANES)
            ref, target = (
                (penalty.at[:, :, z], pen.at[h, own_x, own_y, :]),
                (adjoint.at[:, :, :, z], a_src.at[h, :, own_x, own_y, :]),
                (state.at[:, :, :, z], s_src.at[h, :, own_x, own_y, :]),
            )[k]
            copy = pltpu.make_async_copy(ref, target, load_sem.at[2 * k + h])
            copy.start()
            loads.append(copy)

    zero_margins(s_src)
    peers = 48 + 3 * (has_down.astype(jnp.int32) + has_up.astype(jnp.int32))
    pl.semaphore_wait(barrier, peers)

    def x_copy(which, d, h):
        z, own_y = pl.ds(h * LANES, LANES), pl.ds(Y0, CY)
        if which == FIRST:
            ref, to = first_out.at[d, h], s_src.at[h, :, 14 if d == 0 else 1, own_y, :]
        else:
            rows, target = (pl.ds(0, 2), pl.ds(12, 2)) if d == 0 else (pl.ds(CX - 2, 2), pl.ds(2, 2))
            if which == PEN:
                ref, to = penalty.at[rows, :, z], pen.at[h, target, own_y, :]
            else:
                ref, to = state.at[:, rows, :, z], s_src.at[h, :, target, own_y, :]
        slot = 4 * which if which < FIRST else 12
        return pltpu.make_async_remote_copy(
            src_ref=ref,
            dst_ref=to,
            send_sem=x_send.at[slot + 2 * d + h],
            recv_sem=x_recv.at[slot + 2 * (1 - d) + h],
            device_id=(left if d == 0 else right, n),
            device_id_type=MESH,
        )

    def adjoint_copy(d, h):
        rows = pl.ds(1, OV) if d == 0 else pl.ds(12, OV)
        return pltpu.make_async_remote_copy(
            src_ref=a_b.at[h, :, rows, pl.ds(Y0, CY), :],
            dst_ref=ax_in.at[1 - d, h],
            send_sem=x_send.at[8 + 2 * d + h],
            recv_sem=x_recv.at[8 + 2 * (1 - d) + h],
            device_id=(left if d == 0 else right, n),
            device_id_type=MESH,
        )

    both = [(d, h) for d in (0, 1) for h in (0, 1)]
    for d, h in both:
        x_copy(PEN, d, h).start()

    def y_copy(message, d):
        out, land, rows, side, _ = messages[message]
        return pltpu.make_async_remote_copy(
            src_ref=out.at[d, :, rows, :],
            dst_ref=land.at[1 - d, :, rows, :] if side == 0 else land.at[1 - d, 2 - side],
            send_sem=y_send.at[2 * message + d],
            recv_sem=y_recv.at[2 * message + 1 - d],
            device_id=((w, left, right)[side], down if d == 0 else up),
            device_id_type=MESH,
        )

    messages = (
        (py_out, py_in, pl.ds(0, 24), 0, 0),
        (py_out, pc_in, pl.ds(0, 16), 1, 1),
        (py_out, pc_in, pl.ds(8, 16), 2, 1),
        (sy_out, sy_in, pl.ds(0, 72), 0, 0),
        (sy_out, sc_in, pl.ds(0, 32), 1, 1),
        (sy_out, sc_in, pl.ds(40, 32), 2, 1),
        (ay_out, ay_in, pl.ds(0, 72), 0, 0),
        (ac_out, ac_in, pl.ds(0, 32), 1, 1),
        (ac_out, ac_in, pl.ds(32, 32), 2, 1),
        (pr_out, pr_in, pl.ds(0, 16), 0, 2),
        (sr_out, sr_in, pl.ds(0, 56), 0, 2),
        (ar_out, ar_in, pl.ds(0, 56), 0, 2),
    )

    def each_side(action):
        @pl.when(has_down)
        def _():
            action(0)

        @pl.when(has_up)
        def _():
            action(1)

    def off_chip(action):
        @pl.when(n == 2)
        def _():
            action(0)

        @pl.when(n == 1)
        def _():
            action(1)

    def on_chip(action):
        @pl.when(pc == 1)
        def _():
            action(0)

        @pl.when(pc == 0)
        def _():
            action(1)

    def sides(message):
        return {0: each_side, 1: off_chip, 2: on_chip}[messages[message][4]]

    def y_send_now(message):
        sides(message)(lambda d: y_copy(message, d).start())

    inner = (Y0, Y0 + CY - OV)
    outer = (Y0 - OV, Y0 + CY)

    def rows_of(ref, h, c, i, y):
        return ref.at[h, i, pl.ds(y, OV), :] if c is None else ref.at[h, c, i, pl.ds(y, OV), :]

    def pack(ref, out, start, count, comps, d, ys, base=0):
        def step(k, carry):
            for h in (0, 1):
                for j, c in enumerate(comps):
                    slot = pl.ds(base + (k * len(comps) + j) * OV, OV)
                    out[d, h, slot, :] = rows_of(ref, h, c, start + k, ys[d])[...]
            return carry

        lax.fori_loop(0, count, step, 0)

    def unpack(ref, land, start, count, comps, y, base=0, add=False):
        def step(k, carry):
            for h in (0, 1):
                for j, c in enumerate(comps):
                    slot = pl.ds(base + (k * len(comps) + j) * OV, OV)
                    cell = rows_of(ref, h, c, start + k, y)
                    cell[...] = cell[...] + land[h, slot, :] if add else land[h, slot, :]
            return carry

        lax.fori_loop(0, count, step, 0)

    pen_comps, all_comps = (None,), (0, 1, 2)

    def reduce_copy(use, s, k):
        buffer, base = (total_red, peak_red)[use], 16 * s
        return pltpu.make_async_remote_copy(
            src_ref=buffer.at[base],
            dst_ref=buffer.at[base + k],
            send_sem=r_send.at[2 * use + s],
            recv_sem=r_recv.at[2 * use + s],
            device_id=stages[s][k - 1],
            device_id_type=MESH,
        )

    def reduce_all(use, s):
        count = len(stages[s])
        slots = (total_red, peak_red)[use].at[pl.ds(16 * s + 1, count)]
        return pltpu.make_async_remote_copy(
            src_ref=slots,
            dst_ref=slots,
            send_sem=r_send.at[2 * use + s],
            recv_sem=r_recv.at[2 * use + s],
            device_id=stages[s][0],
            device_id_type=MESH,
        )

    def reduce_start(use, s, value):
        (total_red, peak_red)[use][16 * s] = value
        for k in range(1, len(stages[s]) + 1):
            reduce_copy(use, s, k).start()

    def reduce_finish(use, s, combine):
        reduce_all(use, s).wait_recv()
        value = [(total_red, peak_red)[use][16 * s + k] for k in range(len(stages[s]) + 1)]
        while len(value) > 1:
            value = [combine(value[2 * k], value[2 * k + 1]) for k in range(len(value) // 2)]
        return value[0]

    for copy in loads[:2]:
        copy.wait()
    each_side(lambda d: pack(pen, py_out, X0, CX, pen_comps, d, inner))
    for message in (0, 1, 2):
        y_send_now(message)
    for copy in loads[2:]:
        copy.wait()

    spot = (lax.broadcasted_iota(jnp.int32, (N, W), 0) == n) & (
        lax.broadcasted_iota(jnp.int32, (N, W), 1) == w
    )
    own_group = jnp.sum(jnp.where(spot, owner[...].astype(F32), 0.0), axis=(0, 1), keepdims=True)
    pick = (lax.broadcasted_iota(jnp.int32, (1, LANES), 1).astype(F32) == own_group).astype(F32)
    row = lax.broadcasted_iota(jnp.int32, (8, LANES), 0)
    sums = jnp.zeros((8, LANES), F32)
    for k, ref in enumerate((s_src, a_src)):
        for c in range(3):

            def add(i, total, ref=ref, c=c):
                cells = ref[0, c, i, pl.ds(Y0, CY), :] + ref[1, c, i, pl.ds(Y0, CY), :]
                return total + ((cells[0:8] + cells[8:16]) + (cells[16:24] + cells[24:32]))

            total = lax.fori_loop(X0, X0 + CX, add, jnp.zeros((8, LANES), F32))
            mean = jnp.sum(total, axis=(0, 1), keepdims=True) * (1.0 / (CX * CY * 2 * LANES))
            sums = sums + jnp.where(row == 3 * k + c, mean * pick, 0.0)
    reduce_start(0, 0, sums)

    each_side(lambda d: pack(s_src, sy_out, X0, CX, all_comps, d, inner))
    for message in (3, 4, 5):
        y_send_now(message)
    for d, h in both:
        x_copy(STATE, d, h).start()
    for d, x in ((0, X0 + 2), (1, X0 + CX - OV)):
        for h in (0, 1):
            g = DAMPING / (8.0 + pen[h, x, pl.ds(Y0, CY), :])
            for c in range(3):
                first_out[d, h, c] = g * s_src[h, c, x, pl.ds(Y0, CY), :]
    for d, h in both:
        x_copy(FIRST, d, h).start()

    zero_margins(a_src)
    for ref in (s_a, s_b, a_a, a_b):
        zero_margins(ref)
    zero_rows(a_src, (1, 2, 3, 12, 13, 14))
    zero_rows(a_a, (0, 1, 2, 3, 12, 13, 14, 15))
    zero_rows(a_b, (1, 2, 13, 14))

    width = margin[0, 0]
    column = lax.broadcasted_iota(jnp.int32, (BOX_NY, LANES), 0) + (BOX_Y - Y0)
    place = column + n * CY
    in_y = (column >= -width) & (column < CY + width) & (place >= 0) & (place < N * CY)

    def y_arrived(message, d):
        y_copy(message, 1 - d).wait_recv()

    for d, h in both:
        x_copy(PEN, d, h).wait_recv()
    on_chip(lambda d: pack(pen, pr_out, 2, 2, pen_comps, d, inner))
    on_chip(lambda d: pack(pen, pr_out, 12, 2, pen_comps, d, inner, base=6))
    y_send_now(9)
    for message in (0, 1, 2):
        sides(message)(lambda d, message=message: y_arrived(message, d))
    each_side(lambda d: unpack(pen, py_in.at[d], X0, CX, pen_comps, outer[d]))

    def unpack_penalty(d):
        unpack(pen, pc_in.at[d, 0], 1, OV, pen_comps, outer[d], base=7)
        unpack(pen, pc_in.at[d, 1], 12, OV, pen_comps, outer[d])

    off_chip(unpack_penalty)

    def unpack_relayed_penalty(d):
        y_arrived(9, d)
        unpack(pen, pr_in.at[d], 2, 2, pen_comps, outer[d])
        unpack(pen, pr_in.at[d], 12, 2, pen_comps, outer[d], base=6)

    on_chip(unpack_relayed_penalty)

    def set_gain(i, carry, outermost=False):
        line = jnp.zeros((BOX_NY, LANES), jnp.int32) + (i - X0)
        inside = in_y & (line >= -width) & (line < CX + width)
        for h in (0, 1):
            value = DAMPING / (8.0 + pen[h, i, pl.ds(BOX_Y, BOX_NY), :])
            if outermost:
                value = jnp.where(far, value, 1.0)
            gain[h, i, pl.ds(BOX_Y, BOX_NY), :] = jnp.where(inside, value, 0.0)
        return carry

    spot_y = jnp.zeros((BOX_NY, LANES), jnp.int32) + n
    far = ((spot_y == 1) & (column >= CY)) | ((spot_y == 2) & (column < 0))
    lax.fori_loop(2, XR - 2, set_gain, 0)
    set_gain(1, 0, True)
    set_gain(XR - 2, 0, True)

    def adjoint_first(i, carry):
        for h in (0, 1):
            g = gain[h, i, pl.ds(Y0, CY), :]
            for c in range(3):
                a_a[h, c, i, pl.ds(Y0, CY), :] = g * a_src[h, c, i, pl.ds(Y0, CY), :]
        return carry

    lax.fori_loop(X0, X0 + CX, adjoint_first, 0)
    sweep(a_a, a_b, a_src, gain, 3, 12)
    sweep(a_b, a_a, a_src, gain, 2, 13)
    sweep(a_a, a_b, a_src, gain, 1, 14)
    each_side(lambda d: pack(a_b, ay_out, X0, CX, all_comps, d, outer))
    off_chip(lambda d: pack(a_b, ac_out, 1, OV, all_comps, d, outer))
    off_chip(lambda d: pack(a_b, ac_out, 12, OV, all_comps, d, outer, base=32))
    on_chip(lambda d: pack(a_b, ar_out, 1, OV, all_comps, d, outer))
    on_chip(lambda d: pack(a_b, ar_out, 12, OV, all_comps, d, outer, base=27))
    for message in (11, 6, 7, 8):
        y_send_now(message)

    def add_relayed(d):
        y_arrived(11, d)
        unpack(a_b, ar_in.at[d], 1, OV, all_comps, inner[d], add=True)
        unpack(a_b, ar_in.at[d], 12, OV, all_comps, inner[d], base=27, add=True)

    on_chip(add_relayed)
    for d, h in both:
        adjoint_copy(d, h).start()

    reduce_start(0, 1, reduce_finish(0, 0, jnp.add))

    for d, h in both:
        x_copy(STATE, d, h).wait_recv()
        x_copy(FIRST, d, h).wait_recv()
    on_chip(lambda d: pack(s_src, sr_out, 1, OV, all_comps, d, inner))
    on_chip(lambda d: pack(s_src, sr_out, 12, OV, all_comps, d, inner, base=27))
    y_send_now(10)
    for message in (3, 4, 5):
        sides(message)(lambda d, message=message: y_arrived(message, d))
    each_side(lambda d: unpack(s_src, sy_in.at[d], X0, CX, all_comps, outer[d]))

    def unpack_state(d):
        unpack(s_src, sc_in.at[d, 0], 1, OV, all_comps, outer[d], base=5)
        unpack(s_src, sc_in.at[d, 1], 12, OV, all_comps, outer[d])

    off_chip(unpack_state)

    def unpack_relayed_state(d):
        y_arrived(10, d)
        unpack(s_src, sr_in.at[d], 1, OV, all_comps, outer[d])
        unpack(s_src, sr_in.at[d], 12, OV, all_comps, outer[d], base=27)

    on_chip(unpack_relayed_state)

    def state_first(i, carry):
        for h in (0, 1):
            g = gain[h, i, pl.ds(BOX_Y, BOX_NY), :]
            for c in range(3):
                s_a[h, c, i, pl.ds(BOX_Y, BOX_NY), :] = g * s_src[h, c, i, pl.ds(BOX_Y, BOX_NY), :]
        return carry

    lax.fori_loop(1, XR - 1, state_first, 0)
    sweep(s_a, s_b, s_src, gain, 2, 13)
    sweep(s_b, s_a, s_src, gain, 3, 12)
    sweep(s_a, s_b, s_src, gain, 4, 11, Y0, CY)

    coarse = reduce_finish(0, 1, jnp.add)
    inv = inverse[...]
    across = lax.broadcasted_iota(jnp.int32, (GROUPS, GROUPS), 1)
    along = lax.broadcasted_iota(jnp.int32, (GROUPS, GROUPS), 0)
    rhs = coarse[:, :GROUPS]
    state_row = jnp.sum(
        ((along.astype(F32) == own_group).astype(F32) - 1.0 / GROUPS) * inv, axis=0, keepdims=True
    )
    adjoint_column = jnp.sum(
        (across.astype(F32) == own_group).astype(F32) * inv, axis=1, keepdims=True
    )
    adjoint_row = jnp.sum(jnp.where(along == across, adjoint_column, 0.0), axis=0, keepdims=True)
    centred = rhs - jnp.sum(rhs, axis=1, keepdims=True) * (1.0 / GROUPS)
    by_state = jnp.sum(rhs * state_row, axis=1, keepdims=True)
    by_adjoint = jnp.sum(centred * adjoint_row, axis=1, keepdims=True)
    corr[...] = jnp.where(row < 3, by_state, by_adjoint)

    for message in (6, 7, 8):
        sides(message)(lambda d, message=message: y_arrived(message, d))
    each_side(lambda d: unpack(a_b, ay_in.at[d], X0, CX, all_comps, inner[d], add=True))

    def add_from_side(d):
        unpack(a_b, ac_in.at[d, 0], X0, OV, all_comps, inner[d], add=True)
        unpack(a_b, ac_in.at[d, 1], X0 + CX - OV, OV, all_comps, inner[d], add=True)

    off_chip(add_from_side)

    def correct(i, carry):
        for h in (0, 1):
            z = slice(h * LANES, (h + 1) * LANES)
            for c in range(3):
                state_out[c, i, :, z] = s_b[h, c, X0 + i, pl.ds(Y0, CY), :] + corr[pl.ds(c, 1), :]
                adjoint_out[c, i, :, z] = a_b[h, c, X0 + i, pl.ds(Y0, CY), :] + corr[pl.ds(c + 3, 1), :]
        return carry

    lax.fori_loop(0, CX, correct, 0)

    def product(i, peak, share=None):
        for h in (0, 1):
            z = slice(h * LANES, (h + 1) * LANES)
            raw = None
            for c in range(3):
                a = adjoint_out[c, i, :, z]
                if share is not None:
                    a = a + share[h, c]
                    adjoint_out[c, i, :, z] = a
                s = state_out[c, i, :, z]
                raw = s * a if raw is None else raw + s * a
            sens_out[i, :, z] = -raw
            size = jnp.abs(raw)
            peak = jnp.maximum(
                peak,
                jnp.maximum(jnp.maximum(size[0:8], size[8:16]), jnp.maximum(size[16:24], size[24:32])),
            )
        return peak

    peak = lax.fori_loop(OV, CX - OV, product, jnp.zeros((8, LANES), F32))
    for d, base, outermost in ((0, 0, 2), (1, CX - OV, 0)):
        for h in (0, 1):
            adjoint_copy(1 - d, h).wait_recv()

        def with_share(k, peak, d=d, base=base):
            share = {(h, c): ax_in[d, h, c, k] for h in (0, 1) for c in range(3)}
            return product(base + k, peak, share)

        peak = lax.fori_loop(1 - outermost // 2, OV - outermost // 2, with_share, peak)
        g = [gain[h, X0 + base + outermost, pl.ds(Y0, CY), :] for h in (0, 1)]
        share = {(h, c): g[h] * ax_in[d, h, c, outermost] for h in (0, 1) for c in range(3)}
        peak = product(base + outermost, peak, share)

    reduce_start(1, 0, jnp.max(peak, axis=0, keepdims=True))

    for which in (PEN, STATE, FIRST):
        for d, h in both:
            x_copy(which, d, h).wait_send()
    for d, h in both:
        adjoint_copy(d, h).wait_send()
    for message in range(len(messages)):
        sides(message)(lambda d, message=message: y_copy(message, d).wait_send())
    for s in (0, 1):
        reduce_all(0, s).wait_send()

    reduce_start(1, 1, reduce_finish(1, 0, jnp.maximum))
    reduce_all(1, 0).wait_send()
    peak = reduce_finish(1, 1, jnp.maximum)
    scale = 1.0 / (jnp.max(peak, axis=1, keepdims=True) + PEAK_EPS)

    def normalise(i, carry):
        sens_out[i] = sens_out[i] * scale
        return carry

    lax.fori_loop(0, CX, normalise, 0)
    reduce_all(1, 1).wait_send()


def write_out(state, adjoint, sens, state_out, adjoint_out, sens_out, sem):
    copies = [
        pltpu.make_async_copy(ref, out, sem.at[k])
        for k, (ref, out) in enumerate(
            ((state, state_out), (adjoint, adjoint_out), (sens, sens_out))
        )
    ]
    for copy in copies:
        copy.start()
    for copy in copies:
        copy.wait()


def body(state_rhs, adjoint_rhs, penalty, margin_width, owner_map, coarse_inv):
    vmem = pltpu.VMEM
    field = vmem((2, 3, XR, YR, LANES), F32)
    flat = vmem((2, XR, YR, LANES), F32)

    def message(rows):
        return [vmem((2, 2, rows, LANES), F32)] * 2

    dma = pltpu.SemaphoreType.DMA
    results = pl.pallas_call(
        kernel,
        out_shape=(
            pltpu.VMEM(state_rhs.shape, F32),
            pltpu.VMEM(adjoint_rhs.shape, F32),
            pltpu.VMEM(penalty.shape, F32),
        ),
        in_specs=[pl.BlockSpec(memory_space=pl.ANY)] * 3
        + [pl.BlockSpec(memory_space=pltpu.SMEM)]
        + [pl.BlockSpec(memory_space=vmem)] * 2,
        out_specs=(pl.BlockSpec(memory_space=vmem),) * 3,
        scratch_shapes=[field] * 6
        + [flat] * 2
        + message(24)
        + [vmem((2, 2, 2, 16, LANES), F32)]
        + message(72)
        + [vmem((2, 2, 2, 32, LANES), F32)]
        + message(72)
        + [
            vmem((2, 2, 64, LANES), F32),
            vmem((2, 2, 2, 32, LANES), F32),
        ]
        + message(16)
        + message(56)
        + message(56)
        + [
            vmem((2, 2, 3, OV, CY, LANES), F32),
            vmem((2, 2, 3, CY, LANES), F32),
            vmem((48, 8, LANES), F32),
            vmem((48, 1, LANES), F32),
            vmem((8, LANES), F32),
            dma((6,)),
            dma((16,)),
            dma((16,)),
            dma((24,)),
            dma((24,)),
            dma((4,)),
            dma((4,)),
        ],
        compiler_params=pltpu.CompilerParams(
            collective_id=0, has_side_effects=True, vmem_limit_bytes=56 * 1024 * 1024
        ),
        name="schwarz",
    )(
        pltpu.with_memory_space_constraint(state_rhs, pltpu.HBM),
        pltpu.with_memory_space_constraint(adjoint_rhs, pltpu.HBM),
        pltpu.with_memory_space_constraint(penalty, pltpu.HBM),
        margin_width,
        owner_map.T,
        coarse_inv,
    )
    return pl.pallas_call(
        write_out,
        out_shape=tuple(jax.ShapeDtypeStruct(r.shape, F32) for r in results),
        in_specs=[pl.BlockSpec(memory_space=vmem)] * 3,
        out_specs=(pl.BlockSpec(memory_space=pltpu.HBM),) * 3,
        scratch_shapes=[dma((3,))],
        compiler_params=pltpu.CompilerParams(vmem_limit_bytes=2 * 1024 * 1024),
        name="write_out",
    )(*results)


def solution(mesh):
    placed = (
        P(None, "wide", "narrow", None),
        P(None, "wide", "narrow", None),
        P("wide", "narrow", None),
        P("wide", "narrow"),
        P(),
        P(),
    )
    return jax.shard_map(
        body,
        mesh=mesh,
        in_specs=placed,
        out_specs=(
            P(None, "wide", "narrow", None),
            P(None, "wide", "narrow", None),
            P("wide", "narrow", None),
        ),
        check_vma=False,
    )
```

```python
import functools

import jax
import jax.numpy as jnp
from jax import lax
from jax.experimental import pallas as pl
from jax.experimental.pallas import tpu as pltpu
from jax.sharding import PartitionSpec as P

MESH = pl.DeviceIdType.MESH
F32 = jnp.float32

OV = 3
CX = 8
CY = 32
LANES = 128
GROUPS = 64
W = 128
N = 4
DAMPING = 0.7
PEAK_EPS = 1e-06

XR = 16
YR = 48
X0 = 4
Y0 = 8
BOX_Y = 5
BOX_NY = 40
PEN, STATE, FIRST = 0, 1, 2


def next_and_previous(plus, minus, lane):
    a0, a1 = pltpu.roll(plus[0], LANES - 1, 1), pltpu.roll(plus[1], LANES - 1, 1)
    b0, b1 = pltpu.roll(minus[0], 1, 1), pltpu.roll(minus[1], 1, 1)
    last, first = lane == LANES - 1, lane == 0
    return (
        jnp.where(last, a1, a0) + jnp.where(first, 0.0, b0),
        jnp.where(last, 0.0, a1) + jnp.where(first, b0, b1),
    )


def sweep(src, dst, source, gain, lo, hi, y0=BOX_Y, ny=BOX_NY):
    lane = lax.broadcasted_iota(jnp.int32, (ny, LANES), 1)

    def line(i, carry):
        centre, plus, minus, rest = [], [], [], []
        for h in (0, 1):

            def at(c, di=0, dy=0, h=h):
                return src[h, c, i + di, pl.ds(y0 + dy, ny), :]

            x0, x1, x2 = at(0), at(0, 1), at(0, -1)
            y_0, y1, y2 = at(1), at(1, 0, 1), at(1, 0, -1)
            z0 = at(2)
            xz = 0.25 * (at(2, 1) - at(2, -1))
            yz = 0.25 * (at(2, 0, 1) - at(2, 0, -1))
            zz = 0.25 * ((x1 - x2) + (y1 - y2))
            twice = z0 + z0
            centre.append((x0, y_0, z0))
            plus.append((x0 + xz, y_0 + yz, twice + zz))
            minus.append((x0 - xz, y_0 - yz, twice - zz))
            own_x, own_y = x1 + x2, y1 + y2
            rest.append(
                (
                    (own_x + own_x)
                    + (at(0, 0, 1) + at(0, 0, -1))
                    + 0.25 * ((at(1, 1, 1) - at(1, 1, -1)) - (at(1, -1, 1) - at(1, -1, -1))),
                    (own_y + own_y)
                    + (at(1, 1) + at(1, -1))
                    + 0.25 * ((at(0, 1, 1) - at(0, 1, -1)) - (at(0, -1, 1) - at(0, -1, -1))),
                    (at(2, 1) + at(2, -1)) + (at(2, 0, 1) + at(2, 0, -1)),
                )
            )
        for c in range(3):
            along = next_and_previous((plus[0][c], plus[1][c]), (minus[0][c], minus[1][c]), lane)
            for h in (0, 1):
                total = source[h, c, i, pl.ds(y0, ny), :] + (rest[h][c] + along[h])
                g = gain[h, i, pl.ds(y0, ny), :]
                dst[h, c, i, pl.ds(y0, ny), :] = 0.3 * centre[h][c] + g * total
        return carry

    lax.fori_loop(lo, hi + 1, line, 0)


def zero_rows(ref, rows):
    for i in rows:
        for h in (0, 1):
            for c in range(3):
                ref[h, c, i] = jnp.zeros((YR, LANES), F32)


def zero_margins(ref):
    def one(i, carry):
        for h in (0, 1):
            for y in (0, Y0 + CY):
                if len(ref.shape) == 4:
                    ref[h, i, pl.ds(y, 8), :] = jnp.zeros((8, LANES), F32)
                else:
                    for c in range(3):
                        ref[h, c, i, pl.ds(y, 8), :] = jnp.zeros((8, LANES), F32)
        return carry

    lax.fori_loop(0, XR, one, 0)


def kernel(
    state,
    adjoint,
    penalty,
    margin,
    owner,
    inverse,
    state_out,
    adjoint_out,
    sens_out,
    s_src,
    a_src,
    s_a,
    s_b,
    a_a,
    a_b,
    pen,
    gain,
    py_out,
    py_in,
    pc_in,
    sy_out,
    sy_in,
    sc_in,
    ay_out,
    ay_in,
    ac_out,
    ac_in,
    pr_out,
    pr_in,
    sr_out,
    sr_in,
    ar_out,
    ar_in,
    ax_in,
    first_out,
    total_red,
    peak_red,
    corr,
    load_sem,
    x_send,
    x_recv,
    y_send,
    y_recv,
    r_send,
    r_recv,
):
    w, n = lax.axis_index("wide"), lax.axis_index("narrow")
    py, px, pz = w // 16, lax.rem(w // 4, 4), lax.rem(w, 4)
    ph, pc = n // 2, lax.rem(n, 2)
    left, right = lax.rem(w + W - 1, W), lax.rem(w + 1, W)
    down, up = lax.rem(n + N - 1, N), lax.rem(n + 1, N)
    stages = (
        [
            (py * 16 + px * 4 + lax.rem(pz + k // 4, 4), lax.rem(ph + k // 2 % 2, 2) * 2 + lax.rem(pc + k % 2, 2))
            for k in range(1, 16)
        ],
        [(lax.rem(py + k // 4, 8) * 16 + lax.rem(px + k % 4, 4) * 4 + pz, n) for k in range(1, 32)],
    )
    has_down, has_up = n > 0, n < N - 1

    barrier = pltpu.get_barrier_semaphore()
    for device in [(left, n), (right, n)] + stages[0] + stages[1]:
        pl.semaphore_signal(barrier, inc=1, device_id=device, device_id_type=MESH)

    @pl.when(has_down)
    def _():
        for at in (left, w, right):
            pl.semaphore_signal(barrier, inc=1, device_id=(at, down), device_id_type=MESH)

    @pl.when(has_up)
    def _():
        for at in (left, w, right):
            pl.semaphore_signal(barrier, inc=1, device_id=(at, up), device_id_type=MESH)

    loads = []
    own_x, own_y = pl.ds(X0, CX), pl.ds(Y0, CY)
    for k in range(3):
        for h in (0, 1):
            z = pl.ds(h * LANES, LANES)
            ref, target = (
                (penalty.at[:, :, z], pen.at[h, own_x, own_y, :]),
                (adjoint.at[:, :, :, z], a_src.at[h, :, own_x, own_y, :]),
                (state.at[:, :, :, z], s_src.at[h, :, own_x, own_y, :]),
            )[k]
            copy = pltpu.make_async_copy(ref, target, load_sem.at[2 * k + h])
            copy.start()
            loads.append(copy)

    zero_margins(s_src)
    peers = 48 + 3 * (has_down.astype(jnp.int32) + has_up.astype(jnp.int32))
    pl.semaphore_wait(barrier, peers)

    def x_copy(which, d, h):
        z, own_y = pl.ds(h * LANES, LANES), pl.ds(Y0, CY)
        if which == FIRST:
            ref, to = first_out.at[d, h], s_src.at[h, :, 14 if d == 0 else 1, own_y, :]
        else:
            rows, target = (pl.ds(0, 2), pl.ds(12, 2)) if d == 0 else (pl.ds(CX - 2, 2), pl.ds(2, 2))
            if which == PEN:
                ref, to = penalty.at[rows, :, z], pen.at[h, target, own_y, :]
            else:
                ref, to = state.at[:, rows, :, z], s_src.at[h, :, target, own_y, :]
        slot = 4 * which if which < FIRST else 12
        return pltpu.make_async_remote_copy(
            src_ref=ref,
            dst_ref=to,
            send_sem=x_send.at[slot + 2 * d + h],
            recv_sem=x_recv.at[slot + 2 * (1 - d) + h],
            device_id=(left if d == 0 else right, n),
            device_id_type=MESH,
        )

    def adjoint_copy(d, h):
        rows = pl.ds(1, OV) if d == 0 else pl.ds(12, OV)
        return pltpu.make_async_remote_copy(
            src_ref=a_b.at[h, :, rows, pl.ds(Y0, CY), :],
            dst_ref=ax_in.at[1 - d, h],
            send_sem=x_send.at[8 + 2 * d + h],
            recv_sem=x_recv.at[8 + 2 * (1 - d) + h],
            device_id=(left if d == 0 else right, n),
            device_id_type=MESH,
        )

    both = [(d, h) for d in (0, 1) for h in (0, 1)]
    for d, h in both:
        x_copy(PEN, d, h).start()

    def y_copy(message, d):
        out, land, rows, side, _ = messages[message]
        return pltpu.make_async_remote_copy(
            src_ref=out.at[d, :, rows, :],
            dst_ref=land.at[1 - d, :, rows, :] if side == 0 else land.at[1 - d, 2 - side],
            send_sem=y_send.at[2 * message + d],
            recv_sem=y_recv.at[2 * message + 1 - d],
            device_id=((w, left, right)[side], down if d == 0 else up),
            device_id_type=MESH,
        )

    messages = (
        (py_out, py_in, pl.ds(0, 24), 0, 0),
        (py_out, pc_in, pl.ds(0, 16), 1, 1),
        (py_out, pc_in, pl.ds(8, 16), 2, 1),
        (sy_out, sy_in, pl.ds(0, 72), 0, 0),
        (sy_out, sc_in, pl.ds(0, 32), 1, 1),
        (sy_out, sc_in, pl.ds(40, 32), 2, 1),
        (ay_out, ay_in, pl.ds(0, 72), 0, 0),
        (ac_out, ac_in, pl.ds(0, 32), 1, 1),
        (ac_out, ac_in, pl.ds(32, 32), 2, 1),
        (pr_out, pr_in, pl.ds(0, 16), 0, 2),
        (sr_out, sr_in, pl.ds(0, 56), 0, 2),
        (ar_out, ar_in, pl.ds(0, 56), 0, 2),
    )

    def each_side(action):
        @pl.when(has_down)
        def _():
            action(0)

        @pl.when(has_up)
        def _():
            action(1)

    def off_chip(action):
        @pl.when(n == 2)
        def _():
            action(0)

        @pl.when(n == 1)
        def _():
            action(1)

    def on_chip(action):
        @pl.when(pc == 1)
        def _():
            action(0)

        @pl.when(pc == 0)
        def _():
            action(1)

    def sides(message):
        return {0: each_side, 1: off_chip, 2: on_chip}[messages[message][4]]

    def y_send_now(message):
        sides(message)(lambda d: y_copy(message, d).start())

    inner = (Y0, Y0 + CY - OV)
    outer = (Y0 - OV, Y0 + CY)

    def rows_of(ref, h, c, i, y):
        return ref.at[h, i, pl.ds(y, OV), :] if c is None else ref.at[h, c, i, pl.ds(y, OV), :]

    def pack(ref, out, start, count, comps, d, ys, base=0):
        def step(k, carry):
            for h in (0, 1):
                for j, c in enumerate(comps):
                    slot = pl.ds(base + (k * len(comps) + j) * OV, OV)
                    out[d, h, slot, :] = rows_of(ref, h, c, start + k, ys[d])[...]
            return carry

        lax.fori_loop(0, count, step, 0)

    def unpack(ref, land, start, count, comps, y, base=0, add=False):
        def step(k, carry):
            for h in (0, 1):
                for j, c in enumerate(comps):
                    slot = pl.ds(base + (k * len(comps) + j) * OV, OV)
                    cell = rows_of(ref, h, c, start + k, y)
                    cell[...] = cell[...] + land[h, slot, :] if add else land[h, slot, :]
            return carry

        lax.fori_loop(0, count, step, 0)

    pen_comps, all_comps = (None,), (0, 1, 2)

    def reduce_copy(use, s, k):
        buffer, base = (total_red, peak_red)[use], 16 * s
        return pltpu.make_async_remote_copy(
            src_ref=buffer.at[base],
            dst_ref=buffer.at[base + k],
            send_sem=r_send.at[2 * use + s],
            recv_sem=r_recv.at[2 * use + s],
            device_id=stages[s][k - 1],
            device_id_type=MESH,
        )

    def reduce_all(use, s):
        count = len(stages[s])
        slots = (total_red, peak_red)[use].at[pl.ds(16 * s + 1, count)]
        return pltpu.make_async_remote_copy(
            src_ref=slots,
            dst_ref=slots,
            send_sem=r_send.at[2 * use + s],
            recv_sem=r_recv.at[2 * use + s],
            device_id=stages[s][0],
            device_id_type=MESH,
        )

    def reduce_start(use, s, value):
        (total_red, peak_red)[use][16 * s] = value
        for k in range(1, len(stages[s]) + 1):
            reduce_copy(use, s, k).start()

    def reduce_finish(use, s, combine):
        reduce_all(use, s).wait_recv()
        value = [(total_red, peak_red)[use][16 * s + k] for k in range(len(stages[s]) + 1)]
        while len(value) > 1:
            value = [combine(value[2 * k], value[2 * k + 1]) for k in range(len(value) // 2)]
        return value[0]

    for copy in loads[:2]:
        copy.wait()
    each_side(lambda d: pack(pen, py_out, X0, CX, pen_comps, d, inner))
    for message in (0, 1, 2):
        y_send_now(message)
    for copy in loads[2:]:
        copy.wait()

    spot = (lax.broadcasted_iota(jnp.int32, (N, W), 0) == n) & (
        lax.broadcasted_iota(jnp.int32, (N, W), 1) == w
    )
    own_group = jnp.sum(jnp.where(spot, owner[...].astype(F32), 0.0), axis=(0, 1), keepdims=True)
    pick = (lax.broadcasted_iota(jnp.int32, (1, LANES), 1).astype(F32) == own_group).astype(F32)
    row = lax.broadcasted_iota(jnp.int32, (8, LANES), 0)
    sums = jnp.zeros((8, LANES), F32)
    for k, ref in enumerate((s_src, a_src)):
        for c in range(3):

            def add(i, total, ref=ref, c=c):
                cells = ref[0, c, i, pl.ds(Y0, CY), :] + ref[1, c, i, pl.ds(Y0, CY), :]
                return total + ((cells[0:8] + cells[8:16]) + (cells[16:24] + cells[24:32]))

            total = lax.fori_loop(X0, X0 + CX, add, jnp.zeros((8, LANES), F32))
            mean = jnp.sum(total, axis=(0, 1), keepdims=True) * (1.0 / (CX * CY * 2 * LANES))
            sums = sums + jnp.where(row == 3 * k + c, mean * pick, 0.0)
    reduce_start(0, 0, sums)

    each_side(lambda d: pack(s_src, sy_out, X0, CX, all_comps, d, inner))
    for message in (3, 4, 5):
        y_send_now(message)
    for d, h in both:
        x_copy(STATE, d, h).start()
    for d, x in ((0, X0 + 2), (1, X0 + CX - OV)):
        for h in (0, 1):
            g = DAMPING / (8.0 + pen[h, x, pl.ds(Y0, CY), :])
            for c in range(3):
                first_out[d, h, c] = g * s_src[h, c, x, pl.ds(Y0, CY), :]
    for d, h in both:
        x_copy(FIRST, d, h).start()

    zero_margins(a_src)
    for ref in (s_a, s_b, a_a, a_b):
        zero_margins(ref)
    zero_rows(a_src, (1, 2, 3, 12, 13, 14))
    zero_rows(a_a, (0, 1, 2, 3, 12, 13, 14, 15))
    zero_rows(a_b, (1, 2, 13, 14))

    def adjoint_first(i, carry):
        for h in (0, 1):
            g = DAMPING / (8.0 + pen[h, i, pl.ds(Y0, CY), :])
            for c in range(3):
                a_a[h, c, i, pl.ds(Y0, CY), :] = g * a_src[h, c, i, pl.ds(Y0, CY), :]
        return carry

    lax.fori_loop(X0, X0 + CX, adjoint_first, 0)

    width = margin[0, 0]
    column = lax.broadcasted_iota(jnp.int32, (BOX_NY, LANES), 0) + (BOX_Y - Y0)
    place = column + n * CY
    in_y = (column >= -width) & (column < CY + width) & (place >= 0) & (place < N * CY)

    def y_arrived(message, d):
        y_copy(message, 1 - d).wait_recv()

    for d, h in both:
        x_copy(PEN, d, h).wait_recv()
    on_chip(lambda d: pack(pen, pr_out, 2, 2, pen_comps, d, inner))
    on_chip(lambda d: pack(pen, pr_out, 12, 2, pen_comps, d, inner, base=6))
    y_send_now(9)
    for message in (0, 1, 2):
        sides(message)(lambda d, message=message: y_arrived(message, d))
    each_side(lambda d: unpack(pen, py_in.at[d], X0, CX, pen_comps, outer[d]))

    def unpack_penalty(d):
        unpack(pen, pc_in.at[d, 0], 1, OV, pen_comps, outer[d], base=7)
        unpack(pen, pc_in.at[d, 1], 12, OV, pen_comps, outer[d])

    off_chip(unpack_penalty)

    def unpack_relayed_penalty(d):
        y_arrived(9, d)
        unpack(pen, pr_in.at[d], 2, 2, pen_comps, outer[d])
        unpack(pen, pr_in.at[d], 12, 2, pen_comps, outer[d], base=6)

    on_chip(unpack_relayed_penalty)

    def set_gain(i, carry, outermost=False):
        line = jnp.zeros((BOX_NY, LANES), jnp.int32) + (i - X0)
        inside = in_y & (line >= -width) & (line < CX + width)
        for h in (0, 1):
            value = DAMPING / (8.0 + pen[h, i, pl.ds(BOX_Y, BOX_NY), :])
            if outermost:
                value = jnp.where(far, value, 1.0)
            gain[h, i, pl.ds(BOX_Y, BOX_NY), :] = jnp.where(inside, value, 0.0)
        return carry

    spot_y = jnp.zeros((BOX_NY, LANES), jnp.int32) + n
    far = ((spot_y == 1) & (column >= CY)) | ((spot_y == 2) & (column < 0))
    lax.fori_loop(2, XR - 2, set_gain, 0)
    set_gain(1, 0, True)
    set_gain(XR - 2, 0, True)

    sweep(a_a, a_b, a_src, gain, 3, 12)
    sweep(a_b, a_a, a_src, gain, 2, 13)
    sweep(a_a, a_b, a_src, gain, 1, 14)
    each_side(lambda d: pack(a_b, ay_out, X0, CX, all_comps, d, outer))
    off_chip(lambda d: pack(a_b, ac_out, 1, OV, all_comps, d, outer))
    off_chip(lambda d: pack(a_b, ac_out, 12, OV, all_comps, d, outer, base=32))
    on_chip(lambda d: pack(a_b, ar_out, 1, OV, all_comps, d, outer))
    on_chip(lambda d: pack(a_b, ar_out, 12, OV, all_comps, d, outer, base=27))
    for message in (11, 6, 7, 8):
        y_send_now(message)

    def add_relayed(d):
        y_arrived(11, d)
        unpack(a_b, ar_in.at[d], 1, OV, all_comps, inner[d], add=True)
        unpack(a_b, ar_in.at[d], 12, OV, all_comps, inner[d], base=27, add=True)

    on_chip(add_relayed)
    for d, h in both:
        adjoint_copy(d, h).start()

    reduce_start(0, 1, reduce_finish(0, 0, jnp.add))

    for d, h in both:
        x_copy(STATE, d, h).wait_recv()
        x_copy(FIRST, d, h).wait_recv()
    on_chip(lambda d: pack(s_src, sr_out, 1, OV, all_comps, d, inner))
    on_chip(lambda d: pack(s_src, sr_out, 12, OV, all_comps, d, inner, base=27))
    y_send_now(10)
    for message in (3, 4, 5):
        sides(message)(lambda d, message=message: y_arrived(message, d))
    each_side(lambda d: unpack(s_src, sy_in.at[d], X0, CX, all_comps, outer[d]))

    def unpack_state(d):
        unpack(s_src, sc_in.at[d, 0], 1, OV, all_comps, outer[d], base=5)
        unpack(s_src, sc_in.at[d, 1], 12, OV, all_comps, outer[d])

    off_chip(unpack_state)

    def unpack_relayed_state(d):
        y_arrived(10, d)
        unpack(s_src, sr_in.at[d], 1, OV, all_comps, outer[d])
        unpack(s_src, sr_in.at[d], 12, OV, all_comps, outer[d], base=27)

    on_chip(unpack_relayed_state)

    def state_first(i, carry):
        for h in (0, 1):
            g = gain[h, i, pl.ds(BOX_Y, BOX_NY), :]
            for c in range(3):
                s_a[h, c, i, pl.ds(BOX_Y, BOX_NY), :] = g * s_src[h, c, i, pl.ds(BOX_Y, BOX_NY), :]
        return carry

    lax.fori_loop(1, XR - 1, state_first, 0)
    sweep(s_a, s_b, s_src, gain, 2, 13)
    sweep(s_b, s_a, s_src, gain, 3, 12)
    sweep(s_a, s_b, s_src, gain, 4, 11, Y0, CY)

    coarse = reduce_finish(0, 1, jnp.add)
    inv = inverse[...]
    across = lax.broadcasted_iota(jnp.int32, (GROUPS, GROUPS), 1)
    along = lax.broadcasted_iota(jnp.int32, (GROUPS, GROUPS), 0)
    rhs = coarse[:, :GROUPS]
    state_row = jnp.sum(
        ((along.astype(F32) == own_group).astype(F32) - 1.0 / GROUPS) * inv, axis=0, keepdims=True
    )
    adjoint_column = jnp.sum(
        (across.astype(F32) == own_group).astype(F32) * inv, axis=1, keepdims=True
    )
    adjoint_row = jnp.sum(jnp.where(along == across, adjoint_column, 0.0), axis=0, keepdims=True)
    centred = rhs - jnp.sum(rhs, axis=1, keepdims=True) * (1.0 / GROUPS)
    by_state = jnp.sum(rhs * state_row, axis=1, keepdims=True)
    by_adjoint = jnp.sum(centred * adjoint_row, axis=1, keepdims=True)
    corr[...] = jnp.where(row < 3, by_state, by_adjoint)

    for message in (6, 7, 8):
        sides(message)(lambda d, message=message: y_arrived(message, d))
    each_side(lambda d: unpack(a_b, ay_in.at[d], X0, CX, all_comps, inner[d], add=True))

    def add_from_side(d):
        unpack(a_b, ac_in.at[d, 0], X0, OV, all_comps, inner[d], add=True)
        unpack(a_b, ac_in.at[d, 1], X0 + CX - OV, OV, all_comps, inner[d], add=True)

    off_chip(add_from_side)

    def correct(i, carry):
        for h in (0, 1):
            z = slice(h * LANES, (h + 1) * LANES)
            for c in range(3):
                state_out[c, i, :, z] = s_b[h, c, X0 + i, pl.ds(Y0, CY), :] + corr[pl.ds(c, 1), :]
                adjoint_out[c, i, :, z] = a_b[h, c, X0 + i, pl.ds(Y0, CY), :] + corr[pl.ds(c + 3, 1), :]
        return carry

    lax.fori_loop(0, CX, correct, 0)

    def product(i, peak, share=None):
        for h in (0, 1):
            z = slice(h * LANES, (h + 1) * LANES)
            raw = None
            for c in range(3):
                a = adjoint_out[c, i, :, z]
                if share is not None:
                    a = a + share[h, c]
                    adjoint_out[c, i, :, z] = a
                s = state_out[c, i, :, z]
                raw = s * a if raw is None else raw + s * a
            sens_out[i, :, z] = -raw
            size = jnp.abs(raw)
            peak = jnp.maximum(
                peak,
                jnp.maximum(jnp.maximum(size[0:8], size[8:16]), jnp.maximum(size[16:24], size[24:32])),
            )
        return peak

    peak = lax.fori_loop(OV, CX - OV, product, jnp.zeros((8, LANES), F32))
    for d, base, outermost in ((0, 0, 2), (1, CX - OV, 0)):
        for h in (0, 1):
            adjoint_copy(1 - d, h).wait_recv()

        def with_share(k, peak, d=d, base=base):
            share = {(h, c): ax_in[d, h, c, k] for h in (0, 1) for c in range(3)}
            return product(base + k, peak, share)

        peak = lax.fori_loop(1 - outermost // 2, OV - outermost // 2, with_share, peak)
        g = [gain[h, X0 + base + outermost, pl.ds(Y0, CY), :] for h in (0, 1)]
        share = {(h, c): g[h] * ax_in[d, h, c, outermost] for h in (0, 1) for c in range(3)}
        peak = product(base + outermost, peak, share)

    reduce_start(1, 0, jnp.max(peak, axis=0, keepdims=True))

    for which in (PEN, STATE, FIRST):
        for d, h in both:
            x_copy(which, d, h).wait_send()
    for d, h in both:
        adjoint_copy(d, h).wait_send()
    for message in range(len(messages)):
        sides(message)(lambda d, message=message: y_copy(message, d).wait_send())
    for s in (0, 1):
        reduce_all(0, s).wait_send()

    reduce_start(1, 1, reduce_finish(1, 0, jnp.maximum))
    reduce_all(1, 0).wait_send()
    peak = reduce_finish(1, 1, jnp.maximum)
    scale = 1.0 / (jnp.max(peak, axis=1, keepdims=True) + PEAK_EPS)

    def normalise(i, carry):
        sens_out[i] = sens_out[i] * scale
        return carry

    lax.fori_loop(0, CX, normalise, 0)
    reduce_all(1, 1).wait_send()


def write_out(state, adjoint, sens, state_out, adjoint_out, sens_out, sem):
    copies = [
        pltpu.make_async_copy(ref, out, sem.at[k])
        for k, (ref, out) in enumerate(
            ((state, state_out), (adjoint, adjoint_out), (sens, sens_out))
        )
    ]
    for copy in copies:
        copy.start()
    for copy in copies:
        copy.wait()


def body(state_rhs, adjoint_rhs, penalty, margin_width, owner_map, coarse_inv):
    vmem = pltpu.VMEM
    field = vmem((2, 3, XR, YR, LANES), F32)
    flat = vmem((2, XR, YR, LANES), F32)

    def message(rows):
        return [vmem((2, 2, rows, LANES), F32)] * 2

    dma = pltpu.SemaphoreType.DMA
    results = pl.pallas_call(
        kernel,
        out_shape=(
            pltpu.VMEM(state_rhs.shape, F32),
            pltpu.VMEM(adjoint_rhs.shape, F32),
            pltpu.VMEM(penalty.shape, F32),
        ),
        in_specs=[pl.BlockSpec(memory_space=pl.ANY)] * 3
        + [pl.BlockSpec(memory_space=pltpu.SMEM)]
        + [pl.BlockSpec(memory_space=vmem)] * 2,
        out_specs=(pl.BlockSpec(memory_space=vmem),) * 3,
        scratch_shapes=[field] * 6
        + [flat] * 2
        + message(24)
        + [vmem((2, 2, 2, 16, LANES), F32)]
        + message(72)
        + [vmem((2, 2, 2, 32, LANES), F32)]
        + message(72)
        + [
            vmem((2, 2, 64, LANES), F32),
            vmem((2, 2, 2, 32, LANES), F32),
        ]
        + message(16)
        + message(56)
        + message(56)
        + [
            vmem((2, 2, 3, OV, CY, LANES), F32),
            vmem((2, 2, 3, CY, LANES), F32),
            vmem((48, 8, LANES), F32),
            vmem((48, 1, LANES), F32),
            vmem((8, LANES), F32),
            dma((6,)),
            dma((16,)),
            dma((16,)),
            dma((24,)),
            dma((24,)),
            dma((4,)),
            dma((4,)),
        ],
        compiler_params=pltpu.CompilerParams(
            collective_id=0, has_side_effects=True, vmem_limit_bytes=56 * 1024 * 1024
        ),
        name="schwarz",
    )(
        pltpu.with_memory_space_constraint(state_rhs, pltpu.HBM),
        pltpu.with_memory_space_constraint(adjoint_rhs, pltpu.HBM),
        pltpu.with_memory_space_constraint(penalty, pltpu.HBM),
        margin_width,
        owner_map.T,
        coarse_inv,
    )
    return pl.pallas_call(
        write_out,
        out_shape=tuple(jax.ShapeDtypeStruct(r.shape, F32) for r in results),
        in_specs=[pl.BlockSpec(memory_space=vmem)] * 3,
        out_specs=(pl.BlockSpec(memory_space=pltpu.HBM),) * 3,
        scratch_shapes=[dma((3,))],
        compiler_params=pltpu.CompilerParams(vmem_limit_bytes=2 * 1024 * 1024),
        name="write_out",
    )(*results)


def solution(mesh):
    placed = (
        P(None, "wide", "narrow", None),
        P(None, "wide", "narrow", None),
        P("wide", "narrow", None),
        P("wide", "narrow"),
        P(),
        P(),
    )
    return jax.shard_map(
        body,
        mesh=mesh,
        in_specs=placed,
        out_specs=(
            P(None, "wide", "narrow", None),
            P(None, "wide", "narrow", None),
            P("wide", "narrow", None),
        ),
        check_vma=False,
    )
```
